32 devices in a mesh: seq: 8 (over z, y), head: 4 (over x, core).
Axes of the slice: x: 2, y: 2, z: 4, core: 2. Of those that a mesh axis runs over, the one named last changes fastest.
Arguments:
- queries: bfloat16 [4096, 8192], P('seq', 'head'), may hold values from -6 to 6
- keys: bfloat16 [4096, 8192], P('seq', 'head'), may hold values from -6 to 6
- values: bfloat16 [4096, 8192], P('seq', 'head'), may hold values from -120 to 120
- gate: bfloat16 [4096, 8192], P('seq', 'head'), may hold values from -6 to 6
- grad_out: bfloat16 [4096, 8192], P('seq', 'head'), may hold values from -6 to 6
- gain: float32 [8192], P('head'), may hold values from 0.25 to 1.75
- tile_mask: int32 [32, 4], P('seq'), may hold values from 0 to 1, as said below
Outputs:
- grad_queries: bfloat16 [4096, 8192], P('seq', 'head')
- grad_keys: bfloat16 [4096, 8192], P('seq', 'head')
- grad_values: bfloat16 [4096, 8192], P('seq', 'head')
- grad_gate: bfloat16 [4096, 8192], P('seq', 'head')
- grad_gain: float32 [8192], P('head')
The draws below stay inside these ranges and needn't reach their ends.
Inputs may be any that keep to these rules, and one draw needn't show every extreme that they name: `tile_mask`: entries are 0 or 1; in every slab's 4 x 4 block the diagonal is 1 and entries above it are 0.
All inputs are finite; a program needn't handle non-finite values.
Results may differ from the reference program's by a relative error of at most 0.0058.
Values sent between devices are 32-bit elements; how exact they have to be, the bound alone decides.
No kernel may reach another device: no remote copies, remote signals or barrier semaphores. Data moves between devices by JAX's collectives and lax.ppermute only.
A program may use at most 128 MiB of HBM per device.

```python
import jax
import jax.numpy as jnp
from jax import lax

HEADS = 64
HD = 128
TOK_DEV = 512
TILE = 128
TILES = 4
SLABS = 8
TOKENS = 4096
D = 8192


def draw_values(key, part):
    first, second = jax.random.split(key)
    column_head = (jnp.arange(HEADS * HD) // HD).astype(jnp.float32)
    spread = jax.random.uniform(second, (HEADS * HD,), jnp.float32)
    scale = 3.0 ** (column_head / max(HEADS - 1, 1)) * 10.0 ** spread
    base = jax.random.truncated_normal(first, -4.0, 4.0, (TOKENS, HEADS * HD), jnp.float32)
    return (base * scale[None, :]).astype(jnp.bfloat16)


def draw_tile_mask(key, part):
    picks = jax.random.randint(key, (SLABS * TILES, TILES), 0, 10)
    ones = (picks < 7).astype(jnp.int32)
    row_tile = (jnp.arange(SLABS * TILES) % TILES)[:, None]
    col_tile = jnp.arange(TILES)[None, :]
    lower = col_tile < row_tile
    diagonal = col_tile == row_tile
    return jnp.where(diagonal, 1, jnp.where(lower, ones, 0)).astype(jnp.int32)


def level_of(own_key, shape, cuts, least, largest):
    loudness, own = 1.0, jax.random.fold_in(own_key, 6)
    for axis_at, parts in cuts:
        draws = jnp.exp(jax.random.uniform(jax.random.fold_in(own, axis_at), (parts,), jnp.float32, least / len(cuts), largest / len(cuts)))
        loudness = loudness * jnp.repeat(draws, shape[axis_at] // parts).reshape([-1 if axis == axis_at else 1 for axis in range(len(shape))])
    return loudness


def normal_values(rng, extent, deviation, limit, shards=(), kind=jnp.bfloat16):
    entries = deviation * jax.random.normal(rng, extent, jnp.float32)
    if shards:
        entries = entries * level_of(rng, extent, shards, -0.22, 0.18)
    return jnp.clip(entries, -limit, limit).astype(kind)


def setup_inputs(seed: int = 0) -> dict:
    splits = jax.random.split(jax.random.key(seed), 8)
    return {
        "queries": normal_values(splits[0], (TOKENS, D), 1.0, 6.0, ((0, 8), (1, 4))),
        "keys": normal_values(splits[1], (TOKENS, D), 1.0, 6.0, ((0, 8), (1, 4))),
        "values": draw_values(jax.random.fold_in(splits[7], 71), 0),
        "gate": normal_values(splits[3], (TOKENS, D), 1.5, 6.0, ((0, 8), (1, 4))),
        "grad_out": normal_values(splits[4], (TOKENS, D), 1.0, 6.0, ((0, 8), (1, 4))),
        "gain": jnp.clip(1.0 + 0.15 * jax.random.normal(splits[5], (D,), jnp.float32), 0.25, 1.75),
        "tile_mask": draw_tile_mask(jax.random.fold_in(splits[7], 71), 0),
    }


def round_half(x):
    return lax.optimization_barrier(x.astype(jnp.bfloat16)).astype(jnp.float32)

def keep_mask(tile_rows):
    tiles = tile_rows.shape[0]
    expand = jnp.broadcast_to(tile_rows[:, None, :, None], (tiles, TILE, tiles, TILE)).reshape(TOK_DEV, TOK_DEV) == 1
    place = jnp.arange(TOK_DEV)
    same = place[:, None] // TILE == place[None, :] // TILE
    causal = place[:, None] >= place[None, :]
    return expand & (causal | jnp.logical_not(same))

def reference(queries, keys, values, gate, grad_out, gain, tile_mask):
    f = jnp.float32
    q = queries.astype(f).reshape(SLABS, TOK_DEV, HEADS, HD)
    k = keys.astype(f).reshape(SLABS, TOK_DEV, HEADS, HD)
    v = values.astype(f).reshape(SLABS, TOK_DEV, HEADS, HD)
    masks = tile_mask.reshape(SLABS, TILES, TILES)
    local = jnp.einsum('sthe,sthf->shef', k, v)
    running = jnp.cumsum(local, 0)
    prefix = round_half(jnp.concatenate([jnp.zeros((1, HEADS, HD, HD), f), running[:-1]], 0))

    def forward(item):
        qs, ks, vs, ms, ps = item
        keep = keep_mask(ms)
        scores = jnp.einsum('the,she->hts', qs, ks)
        probs = round_half(jnp.where(keep[None], scores, 0.0))
        return jnp.einsum('hts,shf->thf', probs, vs) + jnp.einsum('the,hef->thf', qs, ps)
    attn = lax.map(forward, (q, k, v, masks, prefix)).reshape(TOKENS, D)
    ms_rows = lax.optimization_barrier(jnp.mean(attn * attn, -1, keepdims=True))
    rms = jnp.sqrt(ms_rows + 1e-06)
    normed = attn / rms
    sig = jax.nn.sigmoid(gate.astype(f))
    upstream = grad_out.astype(f)
    dnorm = upstream * sig
    grad_gate = (upstream * normed * gain * sig * (1.0 - sig)).astype(jnp.bfloat16)
    grad_gain = lax.optimization_barrier(jnp.sum(dnorm * normed, 0))
    cross = lax.optimization_barrier(jnp.mean(dnorm * gain * attn, -1, keepdims=True))
    dattn = round_half((dnorm * gain - attn * cross / (ms_rows + 1e-06)) / rms)
    da = dattn.reshape(SLABS, TOK_DEV, HEADS, HD)
    local_adj = jnp.einsum('sthe,sthf->shef', q, da)
    back = jnp.cumsum(local_adj[::-1], 0)[::-1]
    suffix = round_half(jnp.concatenate([back[1:], jnp.zeros((1, HEADS, HD, HD), f)], 0))

    def backward(item):
        qs, ks, vs, das, ms, ps, ss = item
        keep = keep_mask(ms)
        probs = round_half(jnp.where(keep[None], jnp.einsum('the,she->hts', qs, ks), 0.0))
        dprobs = round_half(jnp.where(keep[None], jnp.einsum('thf,shf->hts', das, vs), 0.0))
        gq = jnp.einsum('hts,she->the', dprobs, ks) + jnp.einsum('thf,hef->the', das, ps)
        gk = jnp.einsum('hts,the->she', dprobs, qs) + jnp.einsum('shf,hef->she', vs, ss)
        gv = jnp.einsum('hts,thf->shf', probs, das) + jnp.einsum('she,hef->shf', ks, ss)
        return (gq.astype(jnp.bfloat16), gk.astype(jnp.bfloat16), gv.astype(jnp.bfloat16))
    gq, gk, gv = lax.map(backward, (q, k, v, da, masks, prefix, suffix))
    return (gq.reshape(TOKENS, D), gk.reshape(TOKENS, D), gv.reshape(TOKENS, D), grad_gate, grad_gain)
```

```python
import functools

import jax
import jax.numpy as jnp
from jax import lax
from jax.experimental import pallas as pl
from jax.experimental.pallas import tpu as pltpu
from jax.sharding import PartitionSpec as P

HD = 128
EPS = 1e-06
F32 = jnp.float32
BF16 = jnp.bfloat16
HIGH = lax.Precision.HIGHEST
VMEM_LIMIT = 32 * 1024 * 1024


def dot(a, b, ca, cb, precision=None):
    return lax.dot_general(
        a, b, (((ca,), (cb,)), ((), ())), precision=precision, preferred_element_type=F32
    )


def call(kernel, name, grid, scalars, ins, in_specs, outs, out_specs, scratch=(), aliases=None, flops=0, moved=0):
    return pl.pallas_call(
        kernel,
        name=name,
        out_shape=outs,
        grid_spec=pltpu.PrefetchScalarGridSpec(
            num_scalar_prefetch=len(scalars),
            grid=grid,
            in_specs=in_specs,
            out_specs=out_specs,
            scratch_shapes=scratch,
        ),
        input_output_aliases=aliases or {},
        cost_estimate=pl.CostEstimate(flops=flops, bytes_accessed=moved, transcendentals=0),
        compiler_params=pltpu.CompilerParams(vmem_limit_bytes=VMEM_LIMIT),
    )(*scalars, *ins)


def head_cols(h):
    return slice(h * HD, (h + 1) * HD)


def load_piece(step, pieces, held):
    for i, piece in enumerate(pieces):

        @pl.when(step == i)
        def _(piece=piece):
            held[...] = piece[...].astype(BF16)


def states_kernel(quad, hs, member, a, b, *outs):
    step = pl.program_id(0)
    sums = [dot(a[:, head_cols(h)], b[:, head_cols(h)], 0, 0) for h in range(hs)]
    for i in range(quad):

        @pl.when(step == i)
        def _(i=i):
            for h in range(hs):
                outs[i][head_cols(h), :] = sums[h]


def masked(scores, row, mask, causal, tile):
    pieces = [scores[:, j * tile : (j + 1) * tile] * mask[row, j].astype(F32) for j in range(row)]
    pieces.append(jnp.where(causal, scores[:, row * tile : (row + 1) * tile], 0.0))
    return jnp.concatenate([piece.astype(BF16) for piece in pieces], 1)


def masked_back(scores, col, tiles, mask, causal, tile):
    pieces = [jnp.where(causal, scores[:, :tile], 0.0)]
    pieces += [
        scores[:, (i - col) * tile : (i - col + 1) * tile] * mask[i, col].astype(F32)
        for i in range(col + 1, tiles)
    ]
    return jnp.concatenate([piece.astype(BF16) for piece in pieces], 1)


def intra_kernel(hs, tiles, tile, mask, q, k, v, gate, up, gain, intra, weight):
    causal = lax.broadcasted_iota(jnp.int32, (tile, tile), 0) >= lax.broadcasted_iota(
        jnp.int32, (tile, tile), 1
    )
    for h in range(hs):
        cols = head_cols(h)
        for i in range(tiles):
            rows = slice(i * tile, (i + 1) * tile)
            seen = slice(0, (i + 1) * tile)
            probs = masked(dot(q[rows, cols], k[seen, cols], 1, 1), i, mask, causal, tile)
            intra[rows, cols] = dot(probs, v[seen, cols], 1, 0)
    sig = jax.nn.sigmoid(gate[...].astype(F32))
    weight[...] = up[...].astype(F32) * sig * gain[...]


def sums_kernel(quad, hs, first, member, q, intra, weight, *rest):
    pieces, rest = rest[:quad], rest[quad:]
    if not first:
        before, rest = rest[0], rest[1:]
    out, held, squares, cross = rest
    step = pl.program_id(0)
    load_piece(step, pieces, held)

    @pl.when(step == 0)
    def _():
        squares[...] = jnp.zeros_like(squares)
        cross[...] = jnp.zeros_like(cross)

    for h in range(hs):
        cols = head_cols(h)
        attn = intra[:, cols] + dot(q[:, cols], held[cols, :], 1, 0)
        squares[...] += attn * attn
        cross[...] += attn * weight[:, cols]

    @pl.when(step == quad - 1)
    def _():
        place = lax.broadcasted_iota(jnp.int32, (8, HD), 0)
        total = dot((place == 0).astype(F32), squares[...], 1, 1, HIGH)
        total = total + dot((place == 1).astype(F32), cross[...], 1, 1, HIGH)
        if not first:
            total = total + before[...]
        out[...] = total


def adjoint_kernel(quad, hs, full, parts_n, member, q, intra, weight, *rest):
    pieces, rest = rest[:quad], rest[quad:]
    parts, rest = rest[:parts_n], rest[parts_n:]
    da, inverse, gains = rest[:3]
    outs = rest[3 : 3 + quad]
    held, factor = rest[3 + quad :]
    step = pl.program_id(0)
    load_piece(step, pieces, held)

    @pl.when(step == 0)
    def _():
        total = parts[0][...]
        for part in parts[1:]:
            total = total + part[...]
        place = lax.broadcasted_iota(jnp.int32, (8, HD), 0)
        squares = dot(total, (place == 0).astype(F32), 0, 0, HIGH)
        cross = dot(total, (place == 1).astype(F32), 0, 0, HIGH)
        mean = squares * (1.0 / full) + EPS
        inverse[...] = lax.rsqrt(mean)
        factor[...] = cross * (1.0 / full) / mean

    adjoints = []
    for h in range(hs):
        cols = head_cols(h)
        attn = intra[:, cols] + dot(q[:, cols], held[cols, :], 1, 0)
        wide = weight[:, cols]
        scale = inverse[...]
        mine = ((wide - attn * factor[...]) * scale).astype(BF16)
        da[:, cols] = mine
        gains[:, cols] = jnp.sum(wide * attn * scale, 0, keepdims=True)
        adjoints.append(dot(q[:, cols], mine, 0, 0))
    for i in range(quad):

        @pl.when(step == i)
        def _(i=i):
            for h in range(hs):
                outs[i][head_cols(h), :] = adjoints[h]


def back_kernel(hs, tiles, tile, steps, olds, member, mask, q, k, v, da, weight, intra, gate, inverse, *rest):
    pieces, rest = rest[:steps], rest[steps + olds :]
    gq, ggate, gk, gv, held = rest
    step = pl.program_id(0)
    load_piece(step, pieces, held)
    row = lax.broadcasted_iota(jnp.int32, (tile, tile), 0)
    col = lax.broadcasted_iota(jnp.int32, (tile, tile), 1)
    causal, causal_back = row >= col, row <= col
    total = tiles * tile
    for h in range(hs):
        cols = head_cols(h)
        prefix = held[cols, :]
        for i in range(tiles):
            rows = slice(i * tile, (i + 1) * tile)
            seen = slice(0, (i + 1) * tile)
            dprobs = masked(dot(da[rows, cols], v[seen, cols], 1, 1), i, mask, causal, tile)
            out = dot(dprobs, k[seen, cols], 1, 0) + dot(da[rows, cols], prefix, 1, 1)
            gq[rows, cols] = out.astype(BF16)
        for j in range(tiles):
            rows = slice(j * tile, (j + 1) * tile)
            later = slice(j * tile, total)
            probs = masked_back(dot(k[rows, cols], q[later, cols], 1, 1), j, tiles, mask, causal_back, tile)
            gv[rows, cols] = dot(probs, da[later, cols], 1, 0)
            dprobs = masked_back(dot(v[rows, cols], da[later, cols], 1, 1), j, tiles, mask, causal_back, tile)
            gk[rows, cols] = dot(dprobs, q[later, cols], 1, 0)
        attn = intra[:, cols] + dot(q[:, cols], prefix, 1, 0)
        sig = jax.nn.sigmoid(gate[:, cols].astype(F32))
        ggate[:, cols] = (weight[:, cols] * attn * inverse[...] * (1.0 - sig)).astype(BF16)


def finish_kernel(quad, hs, olds, member, k, v, gk_part, gv_part, *rest):
    pieces, rest = rest[:quad], rest[quad + olds :]
    gk, gv, held = rest
    load_piece(pl.program_id(0), pieces, held)
    for h in range(hs):
        cols = head_cols(h)
        suffix = held[cols, :]
        gk[:, cols] = (gk_part[:, cols] + dot(v[:, cols], suffix, 1, 1)).astype(BF16)
        gv[:, cols] = (gv_part[:, cols] + dot(k[:, cols], suffix, 1, 0)).astype(BF16)


def scatter(pieces, count):
    return [pieces[0]] + [
        lax.ppermute(pieces[d], "seq", [(b, b ^ d) for b in range(count)]) for d in range(1, len(pieces))
    ]


def carry(pieces, count, later):
    quad = len(pieces)
    total = functools.reduce(jnp.add, pieces)
    groups = count // quad

    def shift(value, by):
        pairs = [(b, b + by * quad) for b in range(count - by * quad)]
        if later:
            pairs = [(t, s) for s, t in pairs]
        return lax.ppermute(value, "seq", pairs)

    if groups == 1:
        return jnp.zeros_like(total)
    total = shift(total, 1)
    by = 1
    while by < groups - 1:
        total = total + shift(total, by)
        by *= 2
    return total


def give_back(pieces, start, count, member, later):
    quad = len(pieces)
    rets = []
    for d in range(quad):
        total = start
        for e in range(quad):
            if e != d:
                source, target = member ^ e, member ^ d
                take = source > target if later else source < target
                total = total + jnp.where(take, pieces[e], 0.0)
        rets.append(total)
    return scatter(rets, count)


def all_sum(value, axis, count):
    by = 1
    while by < count:
        value = value + lax.ppermute(value, axis, [(b, b ^ by) for b in range(count)])
        by *= 2
    return value


def body(queries, keys, values, gate, grad_out, gain, tile_mask):
    rows, width = queries.shape
    heads = width // HD
    tiles = tile_mask.shape[0]
    tile = rows // tiles
    count, sides = lax.axis_size("seq"), lax.axis_size("head")
    quad = next(g for g in (4, 2, 1) if count % g == 0 and heads % g == 0)
    chunks = 2 if heads % (2 * quad) == 0 else 1
    hs = heads // (quad * chunks)
    sw = hs * HD
    cw = quad * sw
    steps = max(1, quad // 2)
    member = lax.rem(lax.axis_index("seq"), quad)
    scalar = member.astype(jnp.int32).reshape(1)
    mask = tile_mask
    gain_row = gain.reshape(1, width)
    full = float(width * sides)

    def block(chunk, base=0):
        return pl.BlockSpec((rows, sw), lambda d, m, *_: (0, chunk * quad + (m[0] ^ (d + base))))

    def whole(shape):
        return pl.BlockSpec(shape, lambda *_: (0,) * len(shape))

    held = pltpu.VMEM((sw, HD), BF16)
    piece, piece_spec = jax.ShapeDtypeStruct((sw, HD), F32), whole((sw, HD))
    any_spec = pl.BlockSpec(memory_space=pl.ANY)
    half = 2 * rows * cw
    product = 2 * rows * HD * HD * quad * hs

    def local_states(c):
        return call(
            functools.partial(states_kernel, quad, hs), "states", (quad,), [scalar], [keys, values],
            [block(c), block(c)], [piece] * quad, [piece_spec] * quad, flops=product, moved=2 * half,
        )

    def intra_part(c):
        plain = pl.BlockSpec((rows, sw), lambda d, m: (0, c * quad + d))
        out = pl.BlockSpec((rows, sw), lambda d, m: (0, d))
        return call(
            functools.partial(intra_kernel, hs, tiles, tile), "intra", (quad,), [mask],
            [queries, keys, values, gate, grad_out, gain_row],
            [plain] * 5 + [pl.BlockSpec((1, sw), lambda d, m: (0, c * quad + d))],
            [jax.ShapeDtypeStruct((rows, cw), F32)] * 2, [out, out], flops=8 * product, moved=9 * half,
        )

    def token_sums(c, intra, weight, prefix, before):
        extra = [] if before is None else [before]
        return call(
            functools.partial(sums_kernel, quad, hs, before is None), "token_sums", (quad,), [scalar],
            [queries, intra, weight, *prefix, *extra],
            [block(c), block(0), block(0)] + [piece_spec] * quad + [whole((8, rows))] * len(extra),
            jax.ShapeDtypeStruct((8, rows), F32), whole((8, rows)),
            [held, pltpu.VMEM((rows, HD), F32), pltpu.VMEM((rows, HD), F32)], flops=product, moved=5 * half,
        )

    def adjoints(c, intra, weight, prefix, parts):
        return call(
            functools.partial(adjoint_kernel, quad, hs, full, sides), "adjoints", (quad,), [scalar],
            [queries, intra, weight, *prefix, *parts],
            [block(c), block(0), block(0)] + [piece_spec] * quad + [whole((8, rows))] * sides,
            [
                jax.ShapeDtypeStruct((rows, cw), BF16),
                jax.ShapeDtypeStruct((rows, HD), F32),
                jax.ShapeDtypeStruct((1, cw), F32),
            ]
            + [piece] * quad,
            [block(0), whole((rows, HD)), pl.BlockSpec((1, sw), lambda d, m: (0, m[0] ^ d))] + [piece_spec] * quad,
            [held, pltpu.VMEM((rows, HD), F32)], flops=2 * product, moved=6 * half,
        )

    def back_part(c, base, intra, weight, da, inverse, prefix, wholes, parts):
        olds = [o for o in [*(wholes or []), *(parts or [])]]
        ins = [queries, keys, values, da, weight, intra, gate, inverse, *prefix[base : base + steps]]
        aliases = {}
        for i, o in enumerate(olds):
            aliases[2 + len(ins) + i] = i
        return call(
            functools.partial(back_kernel, hs, tiles, tile, steps, len(olds)), "back", (steps,), [scalar, mask],
            [*ins, *olds],
            [block(c, base)] * 3 + [block(0, base)] * 3 + [block(c, base), whole((rows, HD))]
            + [piece_spec] * steps + [any_spec] * len(olds),
            [jax.ShapeDtypeStruct((rows, width), BF16)] * 2 + [jax.ShapeDtypeStruct((rows, cw), F32)] * 2,
            [block(c, base)] * 2 + [block(0, base)] * 2,
            [held], aliases, flops=14 * product * steps // quad, moved=12 * half * steps // quad,
        )

    def finish(c, gk_part, gv_part, suffix, olds):
        ins = [keys, values, gk_part, gv_part, *suffix]
        aliases = {1 + len(ins) + i: i for i in range(len(olds))}
        return call(
            functools.partial(finish_kernel, quad, hs, len(olds)), "finish", (quad,), [scalar], [*ins, *olds],
            [block(c)] * 2 + [block(0)] * 2 + [piece_spec] * quad + [any_spec] * len(olds),
            [jax.ShapeDtypeStruct((rows, width), BF16)] * 2, [block(c)] * 2, [held], aliases,
            flops=2 * product, moved=8 * half,
        )

    every = range(chunks)
    gathered = [scatter(local_states(c), count) for c in every]
    intras = [intra_part(c) for c in every]
    carried = [carry(g, count, False) for g in gathered]
    prefix = [give_back(gathered[c], carried[c], count, member, False) for c in every]
    sums = None
    for c in every:
        sums = token_sums(c, *intras[c], prefix[c], sums)
    parts = [sums] + [lax.ppermute(sums, "head", [(b, b ^ d) for b in range(sides)]) for d in range(1, sides)]

    das, gains, gathered = [], [], []
    for c in every:
        da, inverse, gains_c, *pieces = adjoints(c, *intras[c], prefix[c], parts)
        das.append(da)
        gains.append(gains_c)
        gathered.append(scatter(pieces, count))
    gain_sum = all_sum(jnp.concatenate(gains, 1).reshape(width // HD, HD), "seq", count)
    grad_gain = gain_sum.reshape(width) / gain

    wholes, halves = None, []
    for c in every:
        part = None
        for base in range(0, quad, steps):
            gq, ggate, *part = back_part(c, base, *intras[c], das[c], inverse, prefix[c], wholes or [], part)
            wholes = [gq, ggate]
        halves.append(part)
    carried = [carry(g, count, True) for g in gathered]
    suffix = [give_back(gathered[c], carried[c], count, member, True) for c in every]
    outs = []
    for c in every:
        outs = finish(c, *halves[c], suffix[c], outs)
    return wholes[0], outs[0], outs[1], wholes[1], grad_gain


def solution(mesh):
    spec = P("seq", "head")
    return jax.shard_map(
        body, mesh=mesh, in_specs=(spec,) * 5 + (P("head"), P("seq", None)), out_specs=(spec,) * 4 + (P("head"),),
        check_vma=False,
    )
```

```python
import functools

import jax
import jax.numpy as jnp
from jax import lax
from jax.experimental import pallas as pl
from jax.experimental.pallas import tpu as pltpu
from jax.sharding import PartitionSpec as P

HD = 128
EPS = 1e-06
F32 = jnp.float32
BF16 = jnp.bfloat16
HIGH = lax.Precision.HIGHEST
VMEM_LIMIT = 16 * 1024 * 1024
VMEM = pl.BlockSpec(memory_space=pltpu.VMEM)
SMEM = pl.BlockSpec(memory_space=pltpu.SMEM)
HBM = pl.BlockSpec(memory_space=pltpu.HBM)
ANY = pl.BlockSpec(memory_space=pl.ANY)


def dot(a, b, ca, cb, precision=None):
    return lax.dot_general(
        a, b, (((ca,), (cb,)), ((), ())), precision=precision, preferred_element_type=F32
    )


def shape(dims, dtype=F32):
    return jax.ShapeDtypeStruct(dims, dtype)


def call(kernel, name, ins, outs, scratch=(), after=(), aliases=None, flops=0, moved=0):
    after = list(after)

    def run(*refs):
        kernel(*refs[: len(ins)], *refs[len(ins) + len(after) :])

    return pl.pallas_call(
        run,
        name=name,
        out_shape=[o for o, _ in outs],
        in_specs=[s for _, s in ins] + [ANY] * len(after),
        out_specs=[s for _, s in outs],
        scratch_shapes=list(scratch),
        input_output_aliases=aliases or {},
        cost_estimate=pl.CostEstimate(flops=flops, bytes_accessed=moved, transcendentals=0),
        compiler_params=pltpu.CompilerParams(vmem_limit_bytes=VMEM_LIMIT),
    )(*[a for a, _ in ins], *after)


def part(i, size):
    return slice(i * size, (i + 1) * size)


def shard_cols(chunk, quad, d, sw):
    member = lax.rem(lax.axis_index("seq"), quad)
    return pl.ds(pl.multiple_of((chunk * quad + (member ^ d)) * sw, sw), sw)


def masks_kernel(tiles, tile, mask, keep, keep_t):
    row = lax.broadcasted_iota(jnp.int32, (tile, tile), 0)
    col = lax.broadcasted_iota(jnp.int32, (tile, tile), 1)
    for i in range(tiles):
        for j in range(tiles):
            read = mask[i, j] == 1
            if i == j:
                keep[part(i, tile), part(j, tile)] = jnp.where(read & (row >= col), 1.0, 0.0).astype(BF16)
                keep_t[part(j, tile), part(i, tile)] = jnp.where(read & (row <= col), 1.0, 0.0).astype(BF16)
            else:
                value = jnp.where(read & (row >= 0), 1.0, 0.0).astype(BF16)
                keep[part(i, tile), part(j, tile)] = value
                keep_t[part(j, tile), part(i, tile)] = value


def states_kernel(quad, hs, chunk, k, v, k_out, v_out, *rest):
    outs, sems = rest[:quad], rest[quad]
    sw = hs * HD
    copies = []
    for d in range(quad):
        cols = shard_cols(chunk, quad, d, sw)
        pair = [
            pltpu.make_async_copy(src.at[:, cols], dst.at[:, part(d, sw)], sems.at[i, d])
            for i, (src, dst) in enumerate(((k, k_out), (v, v_out)))
        ]
        for copy in pair:
            copy.start()
        copies.append(pair)
    for d in range(quad):
        for copy in copies[d]:
            copy.wait()
        write_states(outs[d], k_out[:, part(d, sw)], v_out[:, part(d, sw)], hs)


def write_states(out, a, b, hs):
    if hs == 2:
        both = dot(a, b, 0, 0)
        for h in range(hs):
            out[part(h, HD), :] = both[part(h, HD), part(h, HD)]
    else:
        for h in range(hs):
            out[part(h, HD), :] = dot(a[:, part(h, HD)], b[:, part(h, HD)], 0, 0)


def intra_kernel(quad, hs, chunk, base, steps, blk, k, v, keep, q, gate, up, gain, intra, weight, q_out, gate_out, up_in, gain_in, sems):
    rows = keep.shape[0]
    sw = hs * HD
    copies = []
    for d in range(steps):
        cols = shard_cols(chunk, quad, base + d, sw)
        group = [
            pltpu.make_async_copy(src.at[:, cols], dst.at[:, part(d, sw)], sems.at[i, d])
            for i, (src, dst) in enumerate(((q, q_out), (gate, gate_out), (up, up_in), (gain, gain_in)))
        ]
        for copy in group:
            copy.start()
        copies.append(group)
    for d in range(steps):
        copies[d][0].wait()
        for h in range(hs):
            mine = part(d * hs + h, HD)
            cols = part((base + d) * hs + h, HD)
            total = None
            for j in range(rows // blk):
                ks, later = part(j, blk), slice(j * blk, rows)
                probs = dot(q_out[later, mine], k[ks, cols], 1, 1).astype(BF16) * keep[later, ks]
                out = dot(probs, v[ks, cols], 1, 0)
                total = out if total is None else jnp.concatenate([total[: j * blk], total[j * blk :] + out], 0)
            intra[:, mine] = total
        for copy in copies[d][1:]:
            copy.wait()
        cols = part(d, sw)
        sig = jax.nn.sigmoid(gate_out[:, cols].astype(F32))
        weight[:, cols] = up_in[:, cols].astype(F32) * sig * gain_in[:, cols]


def sums_kernel(hs, first, sides, pieces_n, *refs):
    queries, intras, weights = refs[:sides], refs[sides : 2 * sides], refs[2 * sides : 3 * sides]
    pieces = refs[3 * sides : 3 * sides + pieces_n]
    rest = refs[3 * sides + pieces_n :]
    before, out = (None, rest[0]) if first else rest
    steps = pieces_n // sides
    squares = cross = None
    for d in range(pieces_n):
        side, at = d // steps, d % steps
        for h in range(hs):
            cols = part(at * hs + h, HD)
            prefix = pieces[d][part(h, HD), :].astype(BF16)
            attn = intras[side][:, cols] + dot(queries[side][:, cols], prefix, 1, 0)
            wide = weights[side][:, cols]
            squares = attn * attn if squares is None else squares + attn * attn
            cross = attn * wide if cross is None else cross + attn * wide
    place = lax.broadcasted_iota(jnp.int32, (8, HD), 0)
    total = dot((place == 0).astype(F32), squares, 1, 1, HIGH)
    total = total + dot((place == 1).astype(F32), cross, 1, 1, HIGH)
    out[...] = total if first else total + before[...]


def adjoint_kernel(hs, full, sides, pieces_n, parts_n, carried, *refs):
    queries, intras, weights = refs[:sides], refs[sides : 2 * sides], refs[2 * sides : 3 * sides]
    refs = refs[3 * sides :]
    pieces, refs = refs[:pieces_n], refs[pieces_n:]
    parts, refs = refs[:parts_n], refs[parts_n:]
    gains_before, refs = refs[: len(carried)], refs[len(carried) :]
    last = carried is not None and len(refs) == 2 + pieces_n + 1
    da, inverse = refs[:2]
    outs = refs[2 : 2 + pieces_n]
    factor = refs[-1]
    total = parts[0][...]
    for one in parts[1:]:
        total = total + one[...]
    place = lax.broadcasted_iota(jnp.int32, (8, HD), 0)
    mean = dot(total, (place == 0).astype(F32), 0, 0, HIGH) * (1.0 / full) + EPS
    inverse[...] = lax.rsqrt(mean)
    factor[...] = dot(total, (place == 1).astype(F32), 0, 0, HIGH) * (1.0 / full) / mean
    steps = pieces_n // sides
    sw = hs * HD
    gains = refs[2 + pieces_n] if not last else None
    for d in range(pieces_n):
        side, at = d // steps, d % steps
        rows_out = []
        for h in range(hs):
            cols = part(at * hs + h, HD)
            prefix = pieces[d][part(h, HD), :].astype(BF16)
            q = queries[side][:, cols]
            attn = intras[side][:, cols] + dot(q, prefix, 1, 0)
            wide = weights[side][:, cols]
            scale = inverse[...]
            da[:, part(d * hs + h, HD)] = ((wide - attn * factor[...]) * scale).astype(BF16)
            rows_out.append(jnp.sum(wide * attn * scale, 0, keepdims=True))
        a = queries[side][:, part(at, sw)]
        write_states(outs[d], a, da[:, part(d, sw)], hs)
        if last:
            older = [g[part(d, hs), :] for g in gains_before]
            filled = len(older) * hs + hs
            pad = outs[d].shape[0] - sw - filled
            zero = [jnp.zeros((pad, HD), F32)] if pad else []
            outs[d][sw:, :] = jnp.concatenate(older + rows_out + zero, 0)
        else:
            gains[part(d, hs), :] = jnp.concatenate(rows_out, 0)


def total_kernel(sw, pieces_n, *refs):
    total = refs[0][...]
    for one in refs[1:pieces_n]:
        total = total + one[...]
    refs[pieces_n][...] = total[:sw]
    if len(refs) > pieces_n + 1:
        refs[pieces_n + 1][...] = total[sw:]


def give_kernel(sw, quad, later, smalls_n, *refs):
    pieces, start, smalls, outs = refs[:quad], refs[quad], refs[quad + 1 : quad + 1 + smalls_n], refs[quad + 1 + smalls_n :]
    member = lax.rem(lax.axis_index("seq"), quad)
    values = [piece[:sw, :] for piece in pieces]
    begin = start[...]
    for d in range(quad):
        total = begin
        for e in range(quad):
            if e != d:
                source, target = member ^ e, member ^ d
                take = source > target if later else source < target
                total = total + values[e] * jnp.where(take, 1.0, 0.0)
        outs[d][:sw, :] = total
    if smalls_n:
        total = smalls[0][...]
        for one in smalls[1:]:
            total = total + one[...]
        for d in range(quad):
            outs[d][sw:, :] = total


def back_kernel(hs, quad, chunk, base, steps, blk, olds, k, v, da, keep, keep_t, q, gate, intra, weight, inverse, *rest):
    pieces, rest = rest[:steps], rest[steps + olds :]
    gq, ggate, gk, gv, gq_out, ggate_out, sems = rest
    rows = keep.shape[0]
    n = rows // blk
    sw = hs * HD
    copies = []
    for d in range(steps):
        for h in range(hs):
            mine = part(d * hs + h, HD)
            cols = part((base + d) * hs + h, HD)
            prefix = pieces[d][part(h, HD), :].astype(BF16)
            total = dot(da[:, cols], prefix, 1, 1)
            for j in range(n):
                ks, later = part(j, blk), slice(j * blk, rows)
                dprobs = dot(da[later, cols], v[ks, cols], 1, 1).astype(BF16) * keep[later, ks]
                out = dot(dprobs, k[ks, cols], 1, 0)
                total = total + out if j == 0 else jnp.concatenate([total[: j * blk], total[j * blk :] + out], 0)
            gq_out[:, mine] = total.astype(BF16)
            sum_k = sum_v = None
            for i in reversed(range(n)):
                qs, end = part(i, blk), (i + 1) * blk
                probs = dot(k[:end, cols], q[qs, mine], 1, 1).astype(BF16) * keep_t[:end, qs]
                add_v = dot(probs, da[qs, cols], 1, 0)
                dprobs = dot(v[:end, cols], da[qs, cols], 1, 1).astype(BF16) * keep_t[:end, qs]
                add_k = dot(dprobs, q[qs, mine], 1, 0)
                if sum_k is None:
                    sum_k, sum_v = add_k, add_v
                else:
                    sum_k = jnp.concatenate([sum_k[:end] + add_k, sum_k[end:]], 0)
                    sum_v = jnp.concatenate([sum_v[:end] + add_v, sum_v[end:]], 0)
            gk[:, mine] = sum_k
            gv[:, mine] = sum_v
            attn = intra[:, mine] + dot(q[:, mine], prefix, 1, 0)
            sig = jax.nn.sigmoid(gate[:, mine].astype(F32))
            ggate_out[:, mine] = (weight[:, mine] * attn * inverse[...] * (1.0 - sig)).astype(BF16)
        cols = shard_cols(chunk, quad, base + d, sw)
        for i, (src, dst) in enumerate(((gq_out, gq), (ggate_out, ggate))):
            copy = pltpu.make_async_copy(src.at[:, part(d, sw)], dst.at[:, cols], sems.at[i, d])
            copy.start()
            copies.append(copy)
    for copy in copies:
        copy.wait()


def finish_kernel(hs, quad, chunk, chunks, sides, olds, last, k, v, *rest):
    gk_parts, gv_parts, rest = rest[:sides], rest[sides : 2 * sides], rest[2 * sides :]
    pieces, rest = rest[:quad], rest[quad:]
    if last:
        gain, rest = rest[0], rest[1:]
    rest = rest[olds:]
    gk, gv, rest = rest[0], rest[1], rest[2:]
    if last:
        ggain, rest = rest[0], rest[1:]
    gk_out, gv_out, sems = rest
    sw = hs * HD
    steps = quad // sides
    copies = []
    for d in range(quad):
        side, at = d // steps, d % steps
        for h in range(hs):
            mine, cols = part(at * hs + h, HD), part(d * hs + h, HD)
            suffix = pieces[d][part(h, HD), :].astype(BF16)
            gk_out[:, cols] = (gk_parts[side][:, mine] + dot(v[:, cols], suffix, 1, 1)).astype(BF16)
            gv_out[:, cols] = (gv_parts[side][:, mine] + dot(k[:, cols], suffix, 1, 0)).astype(BF16)
        cols = shard_cols(chunk, quad, d, sw)
        for i, (src, dst) in enumerate(((gk_out, gk), (gv_out, gv))):
            copy = pltpu.make_async_copy(src.at[:, part(d, sw)], dst.at[:, cols], sems.at[i, d])
            copy.start()
            copies.append(copy)
    if last:
        member = lax.rem(lax.axis_index("seq"), quad)
        for c in range(chunks):
            for d in range(quad):
                for h in range(hs):
                    at = pl.multiple_of(((c * quad + (member ^ d)) * hs + h) * HD, HD)
                    row = sw + c * hs + h
                    ggain[:, pl.ds(at, HD)] = pieces[d][row : row + 1, :] / gain[:, pl.ds(at, HD)]
    for copy in copies:
        copy.wait()


def scatter(pieces, count):
    return [pieces[0]] + [
        lax.ppermute(pieces[d], "seq", [(b, b ^ d) for b in range(count)]) for d in range(1, len(pieces))
    ]


def carry(total, count, quad, later):
    groups = count // quad

    def shift(value, by):
        pairs = [(b, b + by * quad) for b in range(count - by * quad)]
        if later:
            pairs = [(t, s) for s, t in pairs]
        return lax.ppermute(value, "seq", pairs)

    if groups == 1:
        return jnp.zeros_like(total)
    total = shift(total, 1)
    by = 1
    while by < groups - 1:
        total = total + shift(total, by)
        by *= 2
    return total


def body(queries, keys, values, gate, grad_out, gain, tile_mask):
    rows, width = queries.shape
    heads = width // HD
    tiles = tile_mask.shape[0]
    tile = rows // tiles
    blk = 2 * tile if tiles % 2 == 0 else tile
    count, head_n = lax.axis_size("seq"), lax.axis_size("head")
    quad = next(g for g in (4, 2, 1) if count % g == 0 and heads % g == 0)
    chunks = 2 if heads % (2 * quad) == 0 else 1
    hs = heads // (quad * chunks)
    sw = hs * HD
    cw = quad * sw
    sides = 2 if quad % 2 == 0 else 1
    steps = quad // sides
    pw = steps * sw
    pad = -(-chunks * hs // 8) * 8
    every = range(chunks)
    final = chunks - 1
    gain_row = gain.reshape(1, width)
    full = float(width * head_n)
    product = 2 * rows * HD * HD * quad * hs
    half = 2 * rows * cw
    dma = pltpu.SemaphoreType.DMA

    keep, keep_t = call(
        functools.partial(masks_kernel, tiles, tile), "masks", [(tile_mask, SMEM)],
        [(shape((rows, rows), BF16), VMEM)] * 2,
    )

    def states(c, after):
        return call(
            functools.partial(states_kernel, quad, hs, c), "states", [(keys, HBM), (values, HBM)],
            [(shape((rows, cw), BF16), VMEM)] * 2 + [(shape((sw, HD)), VMEM)] * quad,
            [dma((2, quad))], after, flops=product, moved=2 * half,
        )

    def intra(c, side, k, v, after):
        base = side * steps
        return call(
            functools.partial(intra_kernel, quad, hs, c, base, steps, blk), "intra",
            [(k, VMEM), (v, VMEM), (keep, VMEM), (queries, HBM), (gate, HBM), (grad_out, HBM), (gain_row, HBM)],
            [(shape((rows, pw)), VMEM)] * 2 + [(shape((rows, pw), BF16), VMEM)] * 2,
            [pltpu.VMEM((rows, pw), BF16), pltpu.VMEM((1, pw), F32), dma((4, steps))], after,
            flops=4 * product, moved=4 * half,
        )

    def token_sums(lots, prefix, before, after):
        extra = [] if before is None else [(before, VMEM)]
        return call(
            functools.partial(sums_kernel, hs, before is None, sides, quad), "token_sums",
            [(lot[i], VMEM) for i in (2, 0, 1) for lot in lots] + [(p, VMEM) for p in prefix] + extra,
            [(shape((8, rows)), VMEM)], (), after, flops=product, moved=5 * half,
        )[0]

    def adjoints(lots, prefix, parts, gains, last):
        outs = [(shape((rows, cw), BF16), VMEM), (shape((rows, HD)), VMEM)]
        outs += [(shape((sw + (pad if last else 0), HD)), VMEM)] * quad
        if not last:
            outs += [(shape((quad * hs, HD)), VMEM)]
        return call(
            functools.partial(adjoint_kernel, hs, full, sides, quad, head_n, gains), "adjoints",
            [(lot[i], VMEM) for i in (2, 0, 1) for lot in lots] + [(p, VMEM) for p in prefix]
            + [(p, VMEM) for p in parts] + [(g, VMEM) for g in gains],
            outs, [pltpu.VMEM((rows, HD), F32)], flops=2 * product, moved=6 * half,
        )

    def totals(pieces, after):
        small = pieces[0].shape[0] - sw
        return call(
            functools.partial(total_kernel, sw, quad), "total", [(p, VMEM) for p in pieces],
            [(shape((sw, HD)), VMEM)] + ([(shape((small, HD)), VMEM)] if small else []), (), after,
        )

    def give(pieces, start, smalls, later, after):
        size = pieces[0].shape[0]
        return call(
            functools.partial(give_kernel, sw, quad, later, len(smalls)), "give",
            [(p, VMEM) for p in pieces] + [(start, VMEM)] + [(s, VMEM) for s in smalls],
            [(shape((size, HD)), VMEM)] * quad, (), after,
        )

    def back(c, side, k, v, da, lot, inverse, prefix, olds, after):
        base = side * steps
        ins = [(k, VMEM), (v, VMEM), (da, VMEM), (keep, VMEM), (keep_t, VMEM), (lot[2], VMEM), (lot[3], VMEM)]
        ins += [(lot[0], VMEM), (lot[1], VMEM), (inverse, VMEM)]
        ins += [(p, VMEM) for p in prefix[base : base + steps]]
        aliases = {len(ins) + i: i for i in range(len(olds))}
        return call(
            functools.partial(back_kernel, hs, quad, c, base, steps, blk, len(olds)), "back",
            ins + [(o, HBM) for o in olds],
            [(shape((rows, width), BF16), HBM)] * 2 + [(shape((rows, pw)), VMEM)] * 2,
            [pltpu.VMEM((rows, pw), BF16)] * 2 + [dma((2, steps))], after, aliases,
            flops=8 * product, moved=6 * half,
        )

    def finish(c, k, v, lots, suffix, olds, after):
        last = c == final
        ins = [(k, VMEM), (v, VMEM)] + [(lot[i], VMEM) for i in (0, 1) for lot in lots] + [(s, VMEM) for s in suffix]
        ins += [(gain_row, VMEM)] if last else []
        aliases = {len(ins) + i: i for i in range(len(olds))}
        return call(
            functools.partial(finish_kernel, hs, quad, c, chunks, sides, len(olds), last), "finish",
            ins + [(o, HBM) for o in olds],
            [(shape((rows, width), BF16), HBM)] * 2 + ([(shape((1, width)), VMEM)] if last else []),
            [pltpu.VMEM((rows, cw), BF16)] * 2 + [dma((2, quad))], after, aliases,
            flops=2 * product, moved=8 * half,
        )

    def scan(messages, later, jobs):
        met = [scatter(m, count) for m in messages]
        done = jobs[0](messages[-1][:1])
        sums, starts, smalls = [], [], [[] for _ in every]
        for c in every:
            total, *small = totals(met[c], done)
            done = [total]
            sums.append(total)
            starts.append(carry(total, count, quad, later))
            if small:
                groups = count // quad
                smalls[c] = small + [
                    lax.ppermute(small[0], "seq", [(b, (b + s * quad) % count) for b in range(count)])
                    for s in range(1, groups)
                ]
        done = jobs[1](sums[-1:])
        gives = []
        for c in every:
            out = give(met[c], starts[c], smalls[c], later, done)
            done = out[:1]
            gives.append(scatter(out, count))
        return gives, jobs[2](done)

    kv, messages, after = [], [], []
    for c in every:
        k, v, *pieces = states(c, after)
        after = pieces[:1]
        kv.append((k, v))
        messages.append(pieces)
    lots = [[None] * sides for _ in every]
    places = [(c, side) for c in every for side in range(sides)]

    def intra_jobs(picked):
        def run(after):
            for c, side in picked:
                lots[c][side] = intra(c, side, *kv[c], after)
                after = lots[c][side][:1]
            return after

        return run

    def split(make):
        n = len(places)
        return [make(places[: n // 4]), make(places[n // 4 : n - n // 4]), make(places[n - n // 4 :])]

    prefix, after = scan(messages, False, split(intra_jobs))
    sums = None
    for c in every:
        sums = token_sums(lots[c], prefix[c], sums, after)
        after = []
    parts = [sums] + [lax.ppermute(sums, "head", [(b, b ^ d) for b in range(head_n)]) for d in range(1, head_n)]

    das, messages, gains = [], [], []
    for c in every:
        da, inverse, *pieces = adjoints(lots[c], prefix[c], parts, gains if c == final else [], c == final)
        das.append(da)
        messages.append(pieces[:quad])
        gains += pieces[quad:]
    halves = [[None] * sides for _ in every]
    wholes = []

    def back_jobs(picked):
        def run(after):
            for c, side in picked:
                gq, ggate, *own = back(c, side, *kv[c], das[c], lots[c][side], inverse, prefix[c], wholes[-1] if wholes else [], after)
                wholes.append([gq, ggate])
                halves[c][side] = own
                after = own[:1]
            return after

        return run

    suffix, after = scan(messages, True, split(back_jobs))
    outs = []
    for c in every:
        outs = finish(c, *kv[c], halves[c], suffix[c], outs, after)
        after = []
    gq, ggate = wholes[-1]
    return gq, outs[0], outs[1], ggate, outs[2].reshape(width)


def solution(mesh):
    spec = P("seq", "head")
    return jax.shard_map(
        body, mesh=mesh, in_specs=(spec,) * 5 + (P("head"), P("seq", None)), out_specs=(spec,) * 4 + (P("head"),),
        check_vma=False,
    )
```

```python
import functools

import jax
import jax.numpy as jnp
from jax import lax
from jax.experimental import pallas as pl
from jax.experimental.pallas import tpu as pltpu
from jax.sharding import PartitionSpec as P

HD = 128
EPS = 1e-06
F32 = jnp.float32
BF16 = jnp.bfloat16
HIGH = lax.Precision.HIGHEST
VMEM_LIMIT = 16 * 1024 * 1024
VMEM = pl.BlockSpec(memory_space=pltpu.VMEM)
SMEM = pl.BlockSpec(memory_space=pltpu.SMEM)
HBM = pl.BlockSpec(memory_space=pltpu.HBM)
ANY = pl.BlockSpec(memory_space=pl.ANY)
INTRA_SHARE = [1, 0, 2, 0, 1]
BACK_SHARE = [1, 0, 2, 0, 1]
LONG = 1 << 26


def dot(a, b, ca, cb, precision=None):
    return lax.dot_general(
        a, b, (((ca,), (cb,)), ((), ())), precision=precision, preferred_element_type=F32
    )


def shape(dims, dtype=F32):
    return jax.ShapeDtypeStruct(dims, dtype)


def call(kernel, name, ins, outs, scratch=(), after=(), aliases=None, cost=1):
    after = list(after)

    def run(*refs):
        kernel(*refs[: len(ins)], *refs[len(ins) + len(after) :])

    return pl.pallas_call(
        run,
        name=name,
        out_shape=[o for o, _ in outs],
        in_specs=[s for _, s in ins] + [ANY] * len(after),
        out_specs=[s for _, s in outs],
        scratch_shapes=list(scratch),
        input_output_aliases=aliases or {},
        cost_estimate=pl.CostEstimate(flops=cost, bytes_accessed=cost, transcendentals=0),
        compiler_params=pltpu.CompilerParams(vmem_limit_bytes=VMEM_LIMIT),
    )(*[pltpu.with_memory_space_constraint(a, pltpu.HBM) if s is HBM else a for a, s in ins], *after)


def part(i, size):
    return slice(i * size, (i + 1) * size)


def shard_cols(chunk, quad, d, sw):
    member = lax.rem(lax.axis_index("seq"), quad)
    return pl.ds(pl.multiple_of((chunk * quad + (member ^ d)) * sw, sw), sw)


def head_at(chunk, quad, d, hs, h):
    member = lax.rem(lax.axis_index("seq"), quad)
    return pl.ds(pl.multiple_of(((chunk * quad + (member ^ d)) * hs + h) * HD, HD), HD)


def start_fetch(chunk, quad, base, steps, sw, pairs, sems):
    groups = []
    for d in range(steps):
        cols = shard_cols(chunk, quad, base + d, sw)
        group = [
            pltpu.make_async_copy(src.at[:, cols], dst.at[:, part(d, sw)], sems.at[i, d])
            for i, (src, dst) in enumerate(pairs)
        ]
        for copy in group:
            copy.start()
        groups.append(group)
    return groups


def start_store(chunk, quad, base, steps, sw, pairs, sems):
    copies = []
    for d in range(steps):
        cols = shard_cols(chunk, quad, base + d, sw)
        for i, (src, dst) in enumerate(pairs):
            copy = pltpu.make_async_copy(src.at[:, part(d, sw)], dst.at[:, cols], sems.at[i, d])
            copy.start()
            copies.append(copy)
    return copies


def write_masks(tiles, tile, mask, keep, keep_t):
    row = lax.broadcasted_iota(jnp.int32, (tile, tile), 0)
    col = lax.broadcasted_iota(jnp.int32, (tile, tile), 1)
    for i in range(tiles):
        for j in range(tiles):
            read = mask[i, j] == 1
            if i == j:
                keep[part(i, tile), part(j, tile)] = jnp.where(read & (row >= col), 1.0, 0.0).astype(BF16)
                keep_t[part(j, tile), part(i, tile)] = jnp.where(read & (row <= col), 1.0, 0.0).astype(BF16)
            else:
                value = jnp.where(read & (row >= 0), 1.0, 0.0).astype(BF16)
                keep[part(i, tile), part(j, tile)] = value
                keep_t[part(j, tile), part(i, tile)] = value


def states_kernel(quad, hs, chunk, tiles, tile, *refs):
    sw = hs * HD
    first = chunk == 0
    srcs, refs = refs[:2], refs[2:]
    if first:
        mask, refs = refs[0], refs[1:]
    (k_out, v_out), outs, refs = refs[:2], refs[2 : 2 + quad], refs[2 + quad :]
    if first:
        (keep, keep_t), refs = refs[:2], refs[2:]
    groups = start_fetch(chunk, quad, 0, quad, sw, list(zip(srcs, (k_out, v_out))), refs[0])
    if first:
        held, mask_sem = refs[-2:]
        copy = pltpu.make_async_copy(mask, held, mask_sem.at[0])
        copy.start()
        copy.wait()
        write_masks(tiles, tile, held, keep, keep_t)
    for d in range(quad):
        for copy in groups[d]:
            copy.wait()
        write_states(outs[d], k_out[:, part(d, sw)], v_out[:, part(d, sw)], hs)


def write_states(out, a, b, hs):
    if hs == 2:
        both = dot(a, b, 0, 0)
        for h in range(hs):
            out[part(h, HD), :] = both[part(h, HD), part(h, HD)]
    else:
        for h in range(hs):
            out[part(h, HD), :] = dot(a[:, part(h, HD)], b[:, part(h, HD)], 0, 0)


def intra_kernel(quad, hs, chunk, base, steps, blk, k, v, keep, q, gate, up, gain, intra, weight):
    rows = keep.shape[0]
    for d in range(steps):
        for h in range(hs):
            mine = part(d * hs + h, HD)
            cols = part((base + d) * hs + h, HD)
            at = head_at(chunk, quad, base + d, hs, h)
            total = None
            for j in range(rows // blk):
                ks, after = part(j, blk), slice(j * blk, rows)
                probs = dot(q[after, at], k[ks, cols], 1, 1).astype(BF16) * keep[after, ks]
                out = dot(probs, v[ks, cols], 1, 0)
                total = out if total is None else jnp.concatenate([total[: j * blk], total[j * blk :] + out], 0)
            intra[:, mine] = total
            sig = jax.nn.sigmoid(gate[:, at].astype(F32))
            weight[:, mine] = up[:, at].astype(F32) * sig * gain[:, at]


def sums_kernel(hs, chunk, first, sides, pieces_n, q, *refs):
    intras, weights = refs[:sides], refs[sides : 2 * sides]
    pieces = refs[2 * sides : 2 * sides + pieces_n]
    rest = refs[2 * sides + pieces_n :]
    before, out = (None, rest[0]) if first else rest
    steps = pieces_n // sides
    squares = cross = None
    for d in range(pieces_n):
        side, at = d // steps, d % steps
        for h in range(hs):
            cols = part(at * hs + h, HD)
            prefix = pieces[d][part(h, HD), :].astype(BF16)
            attn = intras[side][:, cols] + dot(q[:, head_at(chunk, pieces_n, d, hs, h)], prefix, 1, 0)
            wide = weights[side][:, cols]
            squares = attn * attn if squares is None else squares + attn * attn
            cross = attn * wide if cross is None else cross + attn * wide
    place = lax.broadcasted_iota(jnp.int32, (8, HD), 0)
    total = dot((place == 0).astype(F32), squares, 1, 1, HIGH)
    total = total + dot((place == 1).astype(F32), cross, 1, 1, HIGH)
    out[...] = total if first else total + before[...]


def adjoint_kernel(hs, chunk, full, sides, pieces_n, parts_n, carried, queries, *refs):
    intras, weights = refs[:sides], refs[sides : 2 * sides]
    refs = refs[2 * sides :]
    pieces, refs = refs[:pieces_n], refs[pieces_n:]
    parts, refs = refs[:parts_n], refs[parts_n:]
    gains_before, refs = refs[: len(carried)], refs[len(carried) :]
    last = carried is not None and len(refs) == 2 + pieces_n + 1
    da, inverse = refs[:2]
    outs = refs[2 : 2 + pieces_n]
    factor = refs[-1]
    total = parts[0][...]
    for one in parts[1:]:
        total = total + one[...]
    place = lax.broadcasted_iota(jnp.int32, (8, HD), 0)
    mean = dot(total, (place == 0).astype(F32), 0, 0, HIGH) * (1.0 / full) + EPS
    inverse[...] = lax.rsqrt(mean)
    factor[...] = dot(total, (place == 1).astype(F32), 0, 0, HIGH) * (1.0 / full) / mean
    steps = pieces_n // sides
    sw = hs * HD
    gains = refs[2 + pieces_n] if not last else None
    for d in range(pieces_n):
        side, at = d // steps, d % steps
        rows_out = []
        for h in range(hs):
            cols = part(at * hs + h, HD)
            prefix = pieces[d][part(h, HD), :].astype(BF16)
            q = queries[:, head_at(chunk, pieces_n, d, hs, h)]
            attn = intras[side][:, cols] + dot(q, prefix, 1, 0)
            wide = weights[side][:, cols]
            scale = inverse[...]
            da[:, part(d * hs + h, HD)] = ((wide - attn * factor[...]) * scale).astype(BF16)
            rows_out.append(jnp.sum(wide * attn * scale, 0, keepdims=True))
        a = queries[:, shard_cols(chunk, pieces_n, d, sw)]
        write_states(outs[d], a, da[:, part(d, sw)], hs)
        if last:
            older = [g[part(d, hs), :] for g in gains_before]
            filled = len(older) * hs + hs
            pad = outs[d].shape[0] - sw - filled
            zero = [jnp.zeros((pad, HD), F32)] if pad else []
            outs[d][sw:, :] = jnp.concatenate(older + rows_out + zero, 0)
        else:
            gains[part(d, hs), :] = jnp.concatenate(rows_out, 0)


def total_kernel(sw, pieces_n, whole, *refs):
    total = refs[0][...]
    for one in refs[1:pieces_n]:
        total = total + one[...]
    refs[pieces_n][...] = total if whole else total[:sw]
    if len(refs) > pieces_n + 1:
        refs[pieces_n + 1][...] = total[sw:]


def give_kernel(sw, quad, later, smalls_n, gate_group, *refs):
    pieces, start, smalls, outs = refs[:quad], refs[quad], refs[quad + 1 : quad + 1 + smalls_n], refs[quad + 1 + smalls_n :]
    member = lax.rem(lax.axis_index("seq"), quad)
    values = [piece[:sw, :] for piece in pieces]
    begin = start[:sw, :]
    if gate_group is not None:
        begin = begin * jnp.where(lax.axis_index("seq") // quad == gate_group, 1.0, 0.0)
    for d in range(quad):
        total = begin
        for e in range(quad):
            if e != d:
                source, target = member ^ e, member ^ d
                take = source > target if later else source < target
                total = total + values[e] * jnp.where(take, 1.0, 0.0)
        outs[d][:sw, :] = total
    if smalls_n:
        total = smalls[0][...]
        for one in smalls[1:]:
            total = total + one[...]
        if gate_group is not None:
            total = total + start[sw:, :]
        for d in range(quad):
            outs[d][sw:, :] = total


def back_kernel(hs, quad, chunk, base, steps, blk, before, olds, k, v, da, keep, keep_t, q, gate, intra, weight, inverse, *rest):
    pieces, rest = rest[:steps], rest[steps:]
    olds_in, rest = rest[:2], rest[olds:]
    if before:
        gq, ggate, gk, gv, gq_out, ggate_out, sems = rest
        copies = start_store(*before, hs * HD, list(zip(olds_in, (gq, ggate))), sems)
    else:
        gk, gv, gq_out, ggate_out = rest
        copies = []
    rows = keep.shape[0]
    n = rows // blk
    for d in range(steps):
        for h in range(hs):
            mine = part(d * hs + h, HD)
            cols = part((base + d) * hs + h, HD)
            at = head_at(chunk, quad, base + d, hs, h)
            prefix = pieces[d][part(h, HD), :].astype(BF16)
            total = dot(da[:, cols], prefix, 1, 1)
            for j in range(n):
                ks, later = part(j, blk), slice(j * blk, rows)
                dprobs = dot(da[later, cols], v[ks, cols], 1, 1).astype(BF16) * keep[later, ks]
                out = dot(dprobs, k[ks, cols], 1, 0)
                total = total + out if j == 0 else jnp.concatenate([total[: j * blk], total[j * blk :] + out], 0)
            gq_out[:, mine] = total.astype(BF16)
            sum_k = sum_v = None
            for i in reversed(range(n)):
                qs, end = part(i, blk), (i + 1) * blk
                probs = dot(k[:end, cols], q[qs, at], 1, 1).astype(BF16) * keep_t[:end, qs]
                add_v = dot(probs, da[qs, cols], 1, 0)
                dprobs = dot(v[:end, cols], da[qs, cols], 1, 1).astype(BF16) * keep_t[:end, qs]
                add_k = dot(dprobs, q[qs, at], 1, 0)
                if sum_k is None:
                    sum_k, sum_v = add_k, add_v
                else:
                    sum_k = jnp.concatenate([sum_k[:end] + add_k, sum_k[end:]], 0)
                    sum_v = jnp.concatenate([sum_v[:end] + add_v, sum_v[end:]], 0)
            gk[:, mine] = sum_k
            gv[:, mine] = sum_v
            attn = intra[:, mine] + dot(q[:, at], prefix, 1, 0)
            sig = jax.nn.sigmoid(gate[:, at].astype(F32))
            ggate_out[:, mine] = (weight[:, mine] * attn * inverse[...] * (1.0 - sig)).astype(BF16)
    for copy in copies:
        copy.wait()


def finish_kernel(hs, quad, chunk, chunks, sides, before, olds, last, k, v, *rest):
    gk_parts, gv_parts, rest = rest[:sides], rest[sides : 2 * sides], rest[2 * sides :]
    pieces, rest = rest[:quad], rest[quad:]
    if last:
        gain, rest = rest[0], rest[1:]
    olds_in, rest = rest[:2], rest[olds:]
    gk, gv, rest = rest[0], rest[1], rest[2:]
    if last:
        ggain, rest = rest[0], rest[1:]
    sw = hs * HD
    copies = []
    if before:
        gq, ggate, gk_out, gv_out, sems, old_sems = rest
        copies = start_store(*before, sw, list(zip(olds_in, (gq, ggate))), old_sems)
    else:
        gk_out, gv_out, sems = rest
    for d in range(quad):
        for h in range(hs):
            mine, cols = part(d % (quad // sides) * hs + h, HD), part(d * hs + h, HD)
            suffix = pieces[d][part(h, HD), :].astype(BF16)
            gk_out[:, cols] = (gk_parts[d * sides // quad][:, mine] + dot(v[:, cols], suffix, 1, 1)).astype(BF16)
            gv_out[:, cols] = (gv_parts[d * sides // quad][:, mine] + dot(k[:, cols], suffix, 1, 0)).astype(BF16)
        cols = shard_cols(chunk, quad, d, sw)
        for i, (src, dst) in enumerate(((gk_out, gk), (gv_out, gv))):
            copy = pltpu.make_async_copy(src.at[:, part(d, sw)], dst.at[:, cols], sems.at[i, d])
            copy.start()
            copies.append(copy)
    if last:
        member = lax.rem(lax.axis_index("seq"), quad)
        for c in range(chunks):
            for d in range(quad):
                for h in range(hs):
                    at = pl.multiple_of(((c * quad + (member ^ d)) * hs + h) * HD, HD)
                    row = sw + c * hs + h
                    ggain[:, pl.ds(at, HD)] = pieces[d][row : row + 1, :] / gain[:, pl.ds(at, HD)]
    for copy in copies:
        copy.wait()


def scatter(pieces, count):
    return [pieces[0]] + [
        lax.ppermute(pieces[d], "seq", [(b, b ^ d) for b in range(count)]) for d in range(1, len(pieces))
    ]


def carry(total, count, quad, later):
    groups = count // quad

    def shift(value, by):
        pairs = [(b, b + by * quad) for b in range(count - by * quad)]
        if later:
            pairs = [(t, s) for s, t in pairs]
        return lax.ppermute(value, "seq", pairs)

    if groups == 1:
        return jnp.zeros_like(total)
    total = shift(total, 1)
    by = 1
    while by < groups - 1:
        total = total + shift(total, by)
        by *= 2
    return total


def body(queries, keys, values, gate, grad_out, gain, tile_mask):
    rows, width = queries.shape
    heads = width // HD
    tiles = tile_mask.shape[0]
    tile = rows // tiles
    blk = 2 * tile if tiles % 2 == 0 else tile
    count, head_n = lax.axis_size("seq"), lax.axis_size("head")
    quad = next(g for g in (4, 2, 1) if count % g == 0 and heads % g == 0)
    chunks = 2 if heads % (2 * quad) == 0 else 1
    hs = heads // (quad * chunks)
    sw = hs * HD
    cw = quad * sw
    sides = 2 if quad % 2 == 0 else 1
    steps = quad // sides
    pw = steps * sw
    pad = -(-chunks * hs // 8) * 8
    every = range(chunks)
    final = chunks - 1
    gain_row = gain.reshape(1, width)
    full = float(width * head_n)
    dma = pltpu.SemaphoreType.DMA

    places = [(c, side) for c in every for side in range(sides)]

    def states(c, after):
        first = c == 0
        scratch = [dma((2, quad))]
        scratch += [pltpu.SMEM((tiles, tiles), jnp.int32), dma((1,))] if first else []
        return call(
            functools.partial(states_kernel, quad, hs, c, tiles, tile), "states",
            [(keys, HBM), (values, HBM)] + ([(tile_mask, HBM)] if first else []),
            [(shape((rows, cw), BF16), VMEM)] * 2 + [(shape((sw, HD)), VMEM)] * quad
            + ([(shape((rows, rows), BF16), VMEM)] * 2 if first else []),
            scratch, after,
        )

    def intra(c, side, k, v, after):
        return call(
            functools.partial(intra_kernel, quad, hs, c, side * steps, steps, blk), "intra",
            [(k, VMEM), (v, VMEM), (keep, VMEM), (queries, VMEM), (gate, VMEM), (grad_out, VMEM), (gain_row, VMEM)],
            [(shape((rows, pw)), VMEM)] * 2, [], after,
        )

    def token_sums(c, lots, prefix, before, after):
        extra = [] if before is None else [(before, VMEM)]
        return call(
            functools.partial(sums_kernel, hs, c, before is None, sides, quad), "token_sums",
            [(queries, VMEM)] + [(lot[i], VMEM) for i in (0, 1) for lot in lots] + [(p, VMEM) for p in prefix] + extra,
            [(shape((8, rows)), VMEM)], (), after, cost=LONG,
        )[0]

    def adjoints(c, lots, prefix, parts, gains, last):
        outs = [(shape((rows, cw), BF16), VMEM), (shape((rows, HD)), VMEM)]
        outs += [(shape((sw + (pad if last else 0), HD)), VMEM)] * quad
        if not last:
            outs += [(shape((quad * hs, HD)), VMEM)]
        return call(
            functools.partial(adjoint_kernel, hs, c, full, sides, quad, head_n, gains), "adjoints",
            [(queries, VMEM)] + [(lot[i], VMEM) for i in (0, 1) for lot in lots] + [(p, VMEM) for p in prefix]
            + [(p, VMEM) for p in parts] + [(g, VMEM) for g in gains],
            outs, [pltpu.VMEM((rows, HD), F32)],
        )

    def totals(pieces, whole, after):
        size = pieces[0].shape[0]
        small = 0 if whole else size - sw
        return call(
            functools.partial(total_kernel, sw, quad, whole), "total", [(p, VMEM) for p in pieces],
            [(shape((size if whole else sw, HD)), VMEM)] + ([(shape((small, HD)), VMEM)] if small else []), (), after,
        )

    def give(pieces, start, smalls, later, gate_group, after):
        size = pieces[0].shape[0]
        return call(
            functools.partial(give_kernel, sw, quad, later, len(smalls), gate_group), "give",
            [(p, VMEM) for p in pieces] + [(start, VMEM)] + [(s, VMEM) for s in smalls],
            [(shape((size, HD)), VMEM)] * quad, (), after,
        )

    def back(c, base, size, k, v, da, inverse, prefix, before, olds, after):
        lot = lots[c][base // steps]
        ins = [(k, VMEM), (v, VMEM), (da, VMEM), (keep, VMEM), (keep_t, VMEM), (queries, VMEM), (gate, VMEM)]
        ins += [(lot[0], VMEM), (lot[1], VMEM), (inverse, VMEM)]
        ins += [(p, VMEM) for p in prefix[base : base + size]]
        aliases = {len(ins) + 2 + i: i for i in range(len(olds) - 2)}
        return call(
            functools.partial(back_kernel, hs, quad, c, base, size, blk, before, len(olds)), "back",
            ins + [(o, VMEM) for o in olds[:2]] + [(o, HBM) for o in olds[2:]],
            ([(shape((rows, width), BF16), HBM)] * 2 if before else []) + [(shape((rows, size * sw)), VMEM)] * 2
            + [(shape((rows, size * sw), BF16), VMEM)] * 2,
            [dma((2, before[3]))] if before else [], after, aliases,
        )

    def finish(c, k, v, parts, suffix, before, olds, outs, after):
        last = c == final
        ins = [(k, VMEM), (v, VMEM)] + [(p[i], VMEM) for i in (0, 1) for p in parts] + [(s, VMEM) for s in suffix]
        ins += [(gain_row, VMEM)] if last else []
        ins += [(o, VMEM) for o in olds[:2]]
        aliases = {len(ins) + i: i for i in range(len(outs))}
        begun = len(ins) + len(outs)
        after_outs = 2 + last
        aliases.update({begun + i: after_outs + i for i in range(len(olds) - 2)})
        whole = (shape((rows, width), BF16), HBM)
        return call(
            functools.partial(finish_kernel, hs, quad, c, chunks, sides, before, len(olds) + len(outs), last), "finish",
            ins + [(o, HBM) for o in outs] + [(o, HBM) for o in olds[2:]],
            [whole] * 2 + ([(shape((1, width)), VMEM)] if last else []) + ([whole] * 2 if before else []),
            [pltpu.VMEM((rows, cw), BF16)] * 2 + [dma((2, quad))] + ([dma((2, before[3]))] if before else []),
            after, aliases, cost=LONG,
        )

    def scan(messages, later, jobs):
        met = [scatter(m, count) for m in messages]
        done = messages[-1][:1]
        starts, smalls, gates = [], [[] for _ in every], [None for _ in every]
        pair = count == 2 * quad
        for c in every:
            done = jobs(c, done)
            whole = pair and met[c][0].shape[0] > sw
            total, *small = totals(met[c], whole, done)
            done = [total]
            if whole:
                starts.append(lax.ppermute(total, "seq", [(b, b ^ quad) for b in range(count)]))
                smalls[c] = [total[sw:]]
                gates[c] = 0 if later else 1
                continue
            starts.append(carry(total, count, quad, later))
            if small:
                smalls[c] = small + [
                    lax.ppermute(small[0], "seq", [(b, (b + s * quad) % count) for b in range(count)])
                    for s in range(1, count // quad)
                ]
        gives = []
        for c in every:
            done = jobs(chunks + c, done)
            out = give(met[c], starts[c], smalls[c], later, gates[c], done)
            done = out[:1]
            gives.append(scatter(out, count))
        return gives, jobs(2 * chunks, done)

    kv, messages, after = [], [], []
    for c in every:
        k, v, *pieces = states(c, after)
        if c == 0:
            keep, keep_t = pieces[quad : quad + 2]
        pieces = pieces[:quad]
        after = pieces[:1]
        kv.append((k, v))
        messages.append(pieces)
    lots = [[None] * sides for _ in every]
    def lots_of(items, share):
        cuts, total = [], 0
        for one in share:
            total += one
            cuts.append(round(total * len(items) / sum(share)))
        return [items[i:j] for i, j in zip([0] + cuts, cuts)]

    def windows(share):
        if chunks == 2:
            return share
        return [share[0] + share[1], share[2] + share[3], share[4]]

    intra_lots = lots_of(places, windows(INTRA_SHARE))

    def intra_jobs(window, after):
        for c, side in intra_lots[window]:
            lots[c][side] = intra(c, side, *kv[c], after)
            after = lots[c][side][:1]
        return after

    prefix, after = scan(messages, False, intra_jobs)
    sums = None
    for c in every:
        sums = token_sums(c, lots[c], prefix[c], sums, after)
        after = []
    parts = [sums] + [lax.ppermute(sums, "head", [(b, b ^ d) for b in range(head_n)]) for d in range(1, head_n)]

    das, messages, gains = [], [], []
    for c in every:
        da, inverse, *pieces = adjoints(c, lots[c], prefix[c], parts, gains if c == final else [], c == final)
        das.append(da)
        messages.append(pieces[:quad])
        gains += pieces[quad:]
    halves = [[] for _ in every]
    wholes = []
    back_lots = lots_of(places, windows(BACK_SHARE))
    last_place = [None]

    def back_jobs(window, after):
        for c, side in back_lots[window]:
            begun = back(c, side * steps, steps, *kv[c], das[c], inverse, prefix[c], last_place[0], list(wholes), after)
            own, blocks = begun[-4:-2], begun[-2:]
            wholes[:] = [*blocks, *begun[:-4]]
            last_place[0] = (c, quad, side * steps, steps)
            halves[c].append(own)
            after = own[:1]
        return after

    suffix, after = scan(messages, True, back_jobs)
    outs = []
    for c in every:
        begun = c == 0
        done = finish(
            c, *kv[c], halves[c], suffix[c], last_place[0] if begun else None, list(wholes) if begun else [], outs, after
        )
        outs, after = done[:2], []
        if begun:
            gq, ggate = done[-2:]
    return gq, outs[0], outs[1], ggate, done[2].reshape(width)


def solution(mesh):
    spec = P("seq", "head")
    return jax.shard_map(
        body, mesh=mesh, in_specs=(spec,) * 5 + (P("head"), P("seq", None)), out_specs=(spec,) * 4 + (P("head"),),
        check_vma=False,
    )
```

```python
import functools

import jax
import jax.numpy as jnp
from jax import lax
from jax.experimental import pallas as pl
from jax.experimental.pallas import tpu as pltpu
from jax.sharding import PartitionSpec as P

HD = 128
EPS = 1e-06
F32 = jnp.float32
BF16 = jnp.bfloat16
HIGH = lax.Precision.HIGHEST
VMEM_LIMIT = 12 * 1024 * 1024
VMEM = pl.BlockSpec(memory_space=pltpu.VMEM)
SMEM = pl.BlockSpec(memory_space=pltpu.SMEM)
HBM = pl.BlockSpec(memory_space=pltpu.HBM)
ANY = pl.BlockSpec(memory_space=pl.ANY)
INTRA_SHARE = [1, 0, 2, 0, 1]
BACK_SHARE = [2, 2, 2, 0, 2]
BACK_SIZE = 1
LONG = 1 << 26


def dot(a, b, ca, cb, precision=None):
    return lax.dot_general(
        a, b, (((ca,), (cb,)), ((), ())), precision=precision, preferred_element_type=F32
    )


def shape(dims, dtype=F32):
    return jax.ShapeDtypeStruct(dims, dtype)


def call(kernel, name, ins, outs, scratch=(), after=(), aliases=None, cost=1):
    after = list(after)

    def run(*refs):
        kernel(*refs[: len(ins)], *refs[len(ins) + len(after) :])

    return pl.pallas_call(
        run,
        name=name,
        out_shape=[o for o, _ in outs],
        in_specs=[s for _, s in ins] + [ANY] * len(after),
        out_specs=[s for _, s in outs],
        scratch_shapes=list(scratch),
        input_output_aliases=aliases or {},
        cost_estimate=pl.CostEstimate(flops=cost, bytes_accessed=cost, transcendentals=0),
        compiler_params=pltpu.CompilerParams(vmem_limit_bytes=VMEM_LIMIT),
    )(*[pltpu.with_memory_space_constraint(a, pltpu.HBM) if s is HBM else a for a, s in ins], *after)


def part(i, size):
    return slice(i * size, (i + 1) * size)


def shard_cols(chunk, quad, d, sw):
    member = lax.rem(lax.axis_index("seq"), quad)
    return pl.ds(pl.multiple_of((chunk * quad + (member ^ d)) * sw, sw), sw)


def sum_parts(parts):
    return functools.reduce(jnp.add, parts)


def head_at(chunk, quad, d, hs, h):
    member = lax.rem(lax.axis_index("seq"), quad)
    return pl.ds(pl.multiple_of(((chunk * quad + (member ^ d)) * hs + h) * HD, HD), HD)


def start_fetch(chunk, quad, base, steps, sw, pairs, sems):
    groups = []
    for d in range(steps):
        cols = shard_cols(chunk, quad, base + d, sw)
        group = [
            pltpu.make_async_copy(src.at[:, cols], dst.at[:, part(d, sw)], sems.at[i, d])
            for i, (src, dst) in enumerate(pairs)
        ]
        for copy in group:
            copy.start()
        groups.append(group)
    return groups


def write_masks(tiles, tile, mask, keep, keep_t):
    row = lax.broadcasted_iota(jnp.int32, (tile, tile), 0)
    col = lax.broadcasted_iota(jnp.int32, (tile, tile), 1)
    for i in range(tiles):
        for j in range(tiles):
            read = mask[i, j] == 1
            if i == j:
                keep[part(i, tile), part(j, tile)] = jnp.where(read & (row >= col), 1.0, 0.0).astype(BF16)
                keep_t[part(j, tile), part(i, tile)] = jnp.where(read & (row <= col), 1.0, 0.0).astype(BF16)
            else:
                value = jnp.where(read & (row >= 0), 1.0, 0.0).astype(BF16)
                keep[part(i, tile), part(j, tile)] = value
                keep_t[part(j, tile), part(i, tile)] = value


def states_kernel(quad, hs, chunk, tiles, tile, *refs):
    sw = hs * HD
    first = chunk == 0
    srcs, refs = refs[:2], refs[2:]
    if first:
        mask, refs = refs[0], refs[1:]
    (k_out, v_out), outs, refs = refs[:2], refs[2 : 2 + quad], refs[2 + quad :]
    if first:
        (keep, keep_t), refs = refs[:2], refs[2:]
    groups = start_fetch(chunk, quad, 0, quad, sw, list(zip(srcs, (k_out, v_out))), refs[0])
    if first:
        held, mask_sem = refs[-2:]
        copy = pltpu.make_async_copy(mask, held, mask_sem.at[0])
        copy.start()
        copy.wait()
        write_masks(tiles, tile, held, keep, keep_t)
    for d in range(quad):
        for copy in groups[d]:
            copy.wait()
        write_states(outs[d], k_out[:, part(d, sw)], v_out[:, part(d, sw)], hs)


def write_states(out, a, b, hs):
    if hs == 2:
        both = dot(a, b, 0, 0)
        for h in range(hs):
            out[part(h, HD), :] = both[part(h, HD), part(h, HD)]
    else:
        for h in range(hs):
            out[part(h, HD), :] = dot(a[:, part(h, HD)], b[:, part(h, HD)], 0, 0)


def intra_kernel(quad, hs, chunk, base, steps, blk, k, v, keep, q, gate, up, gain, intra, weight):
    rows = keep.shape[0]
    for d in range(steps):
        for h in range(hs):
            mine = part(d * hs + h, HD)
            cols = part((base + d) * hs + h, HD)
            at = head_at(chunk, quad, base + d, hs, h)
            outs = []
            for j in range(rows // blk):
                ks, after = part(j, blk), slice(j * blk, rows)
                probs = dot(q[after, at], k[ks, cols], 1, 1).astype(BF16) * keep[after, ks]
                outs.append(dot(probs, v[ks, cols], 1, 0))
            for i in range(rows // blk):
                intra[part(i, blk), mine] = sum_parts([outs[j][part(i - j, blk)] for j in range(i + 1)])
            sig = jax.nn.sigmoid(gate[:, at].astype(F32))
            weight[:, mine] = up[:, at].astype(F32) * sig * gain[:, at]


def packed_rows(j, blk):
    at = j * (j + 1) // 2 * blk
    return slice(at, at + (j + 1) * blk)


def probs_kernel(hs, quad, chunk, base, steps, blk, k, q, keep_t, probs):
    for d in range(steps):
        for h in range(hs):
            cols = part((base + d) * hs + h, HD)
            at = head_at(chunk, quad, base + d, hs, h)
            for j in range(keep_t.shape[0] // blk):
                qs, end = part(j, blk), (j + 1) * blk
                one = dot(k[:end, cols], q[qs, at], 1, 1).astype(BF16) * keep_t[:end, qs]
                probs[d * hs + h, packed_rows(j, blk), :] = one


def sums_kernel(hs, chunk, first, sides, pieces_n, q, *refs):
    intras, weights = refs[:sides], refs[sides : 2 * sides]
    pieces = refs[2 * sides : 2 * sides + pieces_n]
    rest = refs[2 * sides + pieces_n :]
    before, out, attn_out = (None, *rest) if first else rest
    steps = pieces_n // sides
    squares = cross = None
    for d in range(pieces_n):
        side, at = d // steps, d % steps
        for h in range(hs):
            cols = part(at * hs + h, HD)
            prefix = pieces[d][part(h, HD), :].astype(BF16)
            attn = intras[side][:, cols] + dot(q[:, head_at(chunk, pieces_n, d, hs, h)], prefix, 1, 0)
            attn_out[:, part(d * hs + h, HD)] = attn
            wide = weights[side][:, cols]
            squares = attn * attn if squares is None else squares + attn * attn
            cross = attn * wide if cross is None else cross + attn * wide
    place = lax.broadcasted_iota(jnp.int32, (8, HD), 0)
    total = dot((place == 0).astype(F32), squares, 1, 1, HIGH)
    total = total + dot((place == 1).astype(F32), cross, 1, 1, HIGH)
    out[...] = total if first else total + before[...]


def adjoint_kernel(hs, chunk, full, sides, quad, parts_n, carried, last, queries, attns, *refs):
    weights, refs = refs[:sides], refs[sides:]
    parts, refs = refs[:parts_n], refs[parts_n:]
    gains_before, refs = refs[:carried], refs[carried:]
    da, inverse = refs[:2]
    outs = refs[2 : 2 + quad]
    factor = refs[-1]
    total = parts[0][...]
    for one in parts[1:]:
        total = total + one[...]
    place = lax.broadcasted_iota(jnp.int32, (8, HD), 0)
    mean = dot(total, (place == 0).astype(F32), 0, 0, HIGH) * (1.0 / full) + EPS
    inverse[...] = lax.rsqrt(mean)
    factor[...] = dot(total, (place == 1).astype(F32), 0, 0, HIGH) * (1.0 / full) / mean
    steps = quad // sides
    sw = hs * HD
    for d in range(quad):
        side, at = d // steps, d % steps
        rows_out = []
        for h in range(hs):
            mine = part(d * hs + h, HD)
            attn = attns[:, mine]
            wide = weights[side][:, part(at * hs + h, HD)]
            scale = inverse[...]
            da[:, mine] = ((wide - attn * factor[...]) * scale).astype(BF16)
            rows_out.append(jnp.sum(wide * attn * scale, 0, keepdims=True))
        write_states(outs[d], queries[:, shard_cols(chunk, quad, d, sw)], da[:, part(d, sw)], hs)
        if last:
            older = [g[part(d, hs), :] for g in gains_before]
            pad = outs[d].shape[0] - sw - (len(older) + 1) * hs
            zero = [jnp.zeros((pad, HD), F32)] if pad else []
            outs[d][sw:, :] = jnp.concatenate(older + rows_out + zero, 0)
        else:
            refs[2 + quad][part(d, hs), :] = jnp.concatenate(rows_out, 0)


def total_kernel(sw, pieces_n, whole, *refs):
    total = refs[0][...]
    for one in refs[1:pieces_n]:
        total = total + one[...]
    refs[pieces_n][...] = total if whole else total[:sw]
    if len(refs) > pieces_n + 1:
        refs[pieces_n + 1][...] = total[sw:]


def give_kernel(sw, quad, later, smalls_n, gate_group, *refs):
    pieces, start, smalls, outs = refs[:quad], refs[quad], refs[quad + 1 : quad + 1 + smalls_n], refs[quad + 1 + smalls_n :]
    member = lax.rem(lax.axis_index("seq"), quad)
    values = [piece[:sw, :] for piece in pieces]
    begin = start[:sw, :]
    if gate_group is not None:
        begin = begin * jnp.where(lax.axis_index("seq") // quad == gate_group, 1.0, 0.0)
    for d in range(quad):
        total = begin
        for e in range(quad):
            if e != d:
                source, target = member ^ e, member ^ d
                take = source > target if later else source < target
                total = total + values[e] * jnp.where(take, 1.0, 0.0)
        outs[d][:sw, :] = total
    if smalls_n:
        small = outs[0].shape[0] - sw
        total = smalls[0][-small:, :]
        for one in smalls[1:]:
            total = total + one[...]
        if gate_group is not None:
            total = total + start[sw:, :]
        for d in range(quad):
            outs[d][sw:, :] = total


def back_kernel(hs, quad, chunk, base, at_side, steps, blk, k, v, da, keep, keep_t, q, gate, attns, weight, inverse, probs, *rest):
    pieces, (gq, ggate, gk, gv) = rest[:steps], rest[steps:]
    rows = keep.shape[0]
    n = rows // blk
    for d in range(steps):
        for h in range(hs):
            mine = part(d * hs + h, HD)
            cols = part((base + d) * hs + h, HD)
            at = head_at(chunk, quad, base + d, hs, h)
            in_side = (at_side + d) * hs + h
            prefix = pieces[d][part(h, HD), :].astype(BF16)
            linear = dot(da[:, cols], prefix, 1, 1)
            dprobs = [
                dot(da[j * blk :, cols], v[part(j, blk), cols], 1, 1).astype(BF16) * keep[j * blk :, part(j, blk)]
                for j in range(n)
            ]
            outs = [dot(dprobs[j], k[part(j, blk), cols], 1, 0) for j in range(n)]
            for i in range(n):
                pieces_q = [linear[part(i, blk)]] + [outs[j][part(i - j, blk)] for j in range(i + 1)]
                gq[part(i, blk), mine] = sum_parts(pieces_q).astype(BF16)
            outs_v, outs_k = [], []
            for j in range(n):
                qs, end = part(j, blk), (j + 1) * blk
                outs_v.append(dot(probs[in_side, packed_rows(j, blk), :], da[qs, cols], 1, 0))
                back = dot(v[:end, cols], da[qs, cols], 1, 1).astype(BF16) * keep_t[:end, qs]
                outs_k.append(dot(back, q[qs, at], 1, 0))
            for i in range(n):
                gv[part(i, blk), mine] = sum_parts([outs_v[j][part(i, blk)] for j in range(i, n)])
                gk[part(i, blk), mine] = sum_parts([outs_k[j][part(i, blk)] for j in range(i, n)])
            sig = jax.nn.sigmoid(gate[:, at].astype(F32))
            ggate[:, mine] = (weight[:, part(in_side, HD)] * attns[:, cols] * inverse[...] * (1.0 - sig)).astype(BF16)


def finish_kernel(hs, quad, chunk, chunks, sizes, olds, last, k, v, *rest):
    n = len(sizes)
    sw = hs * HD
    (gq_parts, ggate_parts, gk_parts, gv_parts), rest = [rest[i * n : (i + 1) * n] for i in range(4)], rest[4 * n :]
    pieces, rest = rest[:quad], rest[quad:]
    if last:
        gain, rest = rest[0], rest[1:]
    rest = rest[olds:]
    gq, ggate, gk, gv, rest = *rest[:4], rest[4:]
    if last:
        ggain, rest = rest[0], rest[1:]
    gk_out, gv_out, sems = rest
    copies = []
    where = [(i, at) for i, size in enumerate(sizes) for at in range(size)]

    def store(d, i, src, dst):
        copy = pltpu.make_async_copy(src, dst.at[:, shard_cols(chunk, quad, d, sw)], sems.at[i, d])
        copy.start()
        copies.append(copy)

    for d in range(quad):
        i, at = where[d]
        store(d, 0, gq_parts[i].at[:, part(at, sw)], gq)
        store(d, 1, ggate_parts[i].at[:, part(at, sw)], ggate)
    for d in range(quad):
        i, at = where[d]
        for h in range(hs):
            mine, cols = part(at * hs + h, HD), part(d * hs + h, HD)
            suffix = pieces[d][part(h, HD), :].astype(BF16)
            gk_out[:, cols] = (gk_parts[i][:, mine] + dot(v[:, cols], suffix, 1, 1)).astype(BF16)
            gv_out[:, cols] = (gv_parts[i][:, mine] + dot(k[:, cols], suffix, 1, 0)).astype(BF16)
        store(d, 2, gk_out.at[:, part(d, sw)], gk)
        store(d, 3, gv_out.at[:, part(d, sw)], gv)
    if last:
        for c in range(chunks):
            for d in range(quad):
                for h in range(hs):
                    at = head_at(c, quad, d, hs, h)
                    row = sw + c * hs + h
                    ggain[:, at] = pieces[d][row : row + 1, :] / gain[:, at]
    for copy in copies:
        copy.wait()


def scatter(pieces, count):
    return [pieces[0]] + [
        lax.ppermute(pieces[d], "seq", [(b, b ^ d) for b in range(count)]) for d in range(1, len(pieces))
    ]


def carry(total, count, quad, later):
    groups = count // quad

    def shift(value, by):
        pairs = [(b, b + by * quad) for b in range(count - by * quad)]
        if later:
            pairs = [(t, s) for s, t in pairs]
        return lax.ppermute(value, "seq", pairs)

    if groups == 1:
        return jnp.zeros_like(total)
    total = shift(total, 1)
    by = 1
    while by < groups - 1:
        total = total + shift(total, by)
        by *= 2
    return total


def body(queries, keys, values, gate, grad_out, gain, tile_mask):
    rows, width = queries.shape
    heads = width // HD
    tiles = tile_mask.shape[0]
    tile = rows // tiles
    blk = 2 * tile if tiles % 2 == 0 else tile
    count, head_n = lax.axis_size("seq"), lax.axis_size("head")
    quad = next(g for g in (4, 2, 1) if count % g == 0 and heads % g == 0)
    chunks = 2 if heads % (2 * quad) == 0 else 1
    hs = heads // (quad * chunks)
    sw = hs * HD
    cw = quad * sw
    sides = 2 if quad % 2 == 0 else 1
    steps = quad // sides
    pw = steps * sw
    pad = -(-chunks * hs // 8) * 8
    every = range(chunks)
    final = chunks - 1
    gain_row = gain.reshape(1, width)
    full = float(width * head_n)
    dma = pltpu.SemaphoreType.DMA
    packed = (rows // blk) * (rows // blk + 1) // 2 * blk

    places = [(c, side) for c in every for side in range(sides)]

    def states(c, after):
        first = c == 0
        scratch = [dma((2, quad))]
        scratch += [pltpu.SMEM((tiles, tiles), jnp.int32), dma((1,))] if first else []
        return call(
            functools.partial(states_kernel, quad, hs, c, tiles, tile), "states",
            [(keys, HBM), (values, HBM)] + ([(tile_mask, HBM)] if first else []),
            [(shape((rows, cw), BF16), VMEM)] * 2 + [(shape((sw, HD)), VMEM)] * quad
            + ([(shape((rows, rows), BF16), VMEM)] * 2 if first else []),
            scratch, after,
        )

    def intra(c, side, k, v, after):
        return call(
            functools.partial(intra_kernel, quad, hs, c, side * steps, steps, blk), "intra",
            [(k, VMEM), (v, VMEM), (keep, VMEM), (queries, VMEM), (gate, VMEM), (grad_out, VMEM), (gain_row, VMEM)],
            [(shape((rows, pw)), VMEM)] * 2, [], after,
        )

    def token_sums(c, lots, prefix, before, after):
        extra = [] if before is None else [(before, VMEM)]
        return call(
            functools.partial(sums_kernel, hs, c, before is None, sides, quad), "token_sums",
            [(queries, VMEM)] + [(lot[i], VMEM) for i in (0, 1) for lot in lots] + [(p, VMEM) for p in prefix] + extra,
            [(shape((8, rows)), VMEM), (shape((rows, cw)), VMEM)], (), after, cost=LONG,
        )

    def adjoints(c, attn, parts, gains, after):
        last = c == final
        outs = [(shape((rows, cw), BF16), VMEM), (shape((rows, HD)), VMEM)]
        outs += [(shape((sw + (pad if last else 0), HD)), VMEM)] * quad
        if not last:
            outs += [(shape((quad * hs, HD)), VMEM)]
        return call(
            functools.partial(adjoint_kernel, hs, c, full, sides, quad, head_n, len(gains), last), "adjoints",
            [(queries, VMEM), (attn, VMEM)] + [(lot[1], VMEM) for lot in lots[c]] + [(p, VMEM) for p in parts]
            + [(g, VMEM) for g in gains],
            outs, [pltpu.VMEM((rows, HD), F32)], after,
        )

    def probabilities(c, side, k, after):
        return call(
            functools.partial(probs_kernel, hs, quad, c, side * steps, steps, blk), "probs",
            [(k, VMEM), (queries, VMEM), (keep_t, VMEM)], [(shape((steps * hs, packed, blk), BF16), VMEM)], [], after,
        )[0]

    def totals(pieces, whole, after):
        size = pieces[0].shape[0]
        small = 0 if whole else size - sw
        return call(
            functools.partial(total_kernel, sw, quad, whole), "total", [(p, VMEM) for p in pieces],
            [(shape((size if whole else sw, HD)), VMEM)] + ([(shape((small, HD)), VMEM)] if small else []), (), after,
        )

    def give(pieces, start, smalls, later, gate_group, after):
        size = pieces[0].shape[0]
        return call(
            functools.partial(give_kernel, sw, quad, later, len(smalls), gate_group), "give",
            [(p, VMEM) for p in pieces] + [(start, VMEM)] + [(s, VMEM) for s in smalls],
            [(shape((size, HD)), VMEM)] * quad, (), after,
        )

    def back(c, base, size, k, v, da, inverse, prefix, after):
        side = base // steps
        ins = [(k, VMEM), (v, VMEM), (da, VMEM), (keep, VMEM), (keep_t, VMEM), (queries, VMEM), (gate, VMEM)]
        ins += [(attns[c], VMEM), (lots[c][side][1], VMEM), (inverse, VMEM), (probs[(c, side)], VMEM)]
        ins += [(p, VMEM) for p in prefix[base : base + size]]
        return call(
            functools.partial(back_kernel, hs, quad, c, base, base % steps, size, blk), "back", ins,
            [(shape((rows, size * sw), BF16), VMEM)] * 2 + [(shape((rows, size * sw)), VMEM)] * 2, [], after,
        )

    def finish(c, k, v, suffix, outs, after):
        last = c == final
        parts = halves[c]
        ins = [(k, VMEM), (v, VMEM)] + [(p[i], VMEM) for i in range(4) for p in parts] + [(s, VMEM) for s in suffix]
        ins += [(gain_row, VMEM)] if last else []
        aliases = {len(ins) + i: i for i in range(len(outs))}
        sizes = tuple(p[0].shape[1] // sw for p in parts)
        return call(
            functools.partial(finish_kernel, hs, quad, c, chunks, sizes, len(outs), last), "finish",
            ins + [(o, HBM) for o in outs],
            [(shape((rows, width), BF16), HBM)] * 4 + ([(shape((1, width)), VMEM)] if last else []),
            [pltpu.VMEM((rows, cw), BF16)] * 2 + [dma((4, quad))], after, aliases, cost=LONG,
        )

    def scan(messages, later, jobs):
        met = [scatter(m, count) for m in messages]
        done = messages[-1][:1]
        starts, smalls, gates = [], [[] for _ in every], [None for _ in every]
        pair = count == 2 * quad
        for c in every:
            done = jobs(c, done)
            total, *small = totals(met[c], pair, done)
            done = [total]
            if pair:
                starts.append(lax.ppermute(total, "seq", [(b, b ^ quad) for b in range(count)]))
                smalls[c] = [total] if total.shape[0] > sw else []
                gates[c] = 0 if later else 1
                continue
            starts.append(carry(total, count, quad, later))
            if small:
                smalls[c] = small + [
                    lax.ppermute(small[0], "seq", [(b, (b + s * quad) % count) for b in range(count)])
                    for s in range(1, count // quad)
                ]
        gives = []
        for c in every:
            done = jobs(chunks + c, done)
            out = give(met[c], starts[c], smalls[c], later, gates[c], done)
            done = out[:1]
            gives.append(scatter(out, count))
        return gives, jobs(2 * chunks, done)

    kv, messages, after = [], [], []
    for c in every:
        k, v, *pieces = states(c, after)
        if c == 0:
            keep, keep_t = pieces[quad : quad + 2]
        pieces = pieces[:quad]
        after = pieces[:1]
        kv.append((k, v))
        messages.append(pieces)
    lots = [[None] * sides for _ in every]
    def lots_of(items, share):
        cuts, total = [], 0
        for one in share:
            total += one
            cuts.append(round(total * len(items) / sum(share)))
        return [items[i:j] for i, j in zip([0] + cuts, cuts)]

    def windows(share):
        if chunks == 2:
            return share
        return [share[0] + share[1], share[2] + share[3], share[4]]

    intra_lots = lots_of(places, windows(INTRA_SHARE))

    def intra_jobs(window, after):
        for c, side in intra_lots[window]:
            lots[c][side] = intra(c, side, *kv[c], after)
            after = lots[c][side][:1]
        return after

    prefix, after = scan(messages, False, intra_jobs)
    sums, attns = None, []
    for c in every:
        sums, attn = token_sums(c, lots[c], prefix[c], sums, after)
        attns.append(attn)
        after = []
    parts = [sums] + [lax.ppermute(sums, "head", [(b, b ^ d) for b in range(head_n)]) for d in range(1, head_n)]
    after, probs = [sums], {}
    for place in places:
        probs[place] = probabilities(*place, kv[place[0]][0], after)
        after = [probs[place]]

    das, messages, gains = [], [], []
    for c in every:
        da, inverse, *pieces = adjoints(c, attns[c], parts, gains if c == final else [], after)
        after = []
        das.append(da)
        messages.append(pieces[:quad])
        gains += pieces[quad:]
    halves = [[] for _ in every]
    size = min(BACK_SIZE, steps)
    back_lots = lots_of([(c, d) for c in every for d in range(0, quad, size)], windows(BACK_SHARE))

    def back_jobs(window, after):
        for c, d in back_lots[window]:
            halves[c].append(back(c, d, size, *kv[c], das[c], inverse, prefix[c], after))
            after = halves[c][-1][2:3]
        return after

    suffix, after = scan(messages, True, back_jobs)
    outs = []
    for c in every:
        outs = finish(c, *kv[c], suffix[c], outs[:4], after)
        after = []
    gq, ggate, gk, gv, ggain = outs
    return gq, gk, gv, ggate, ggain.reshape(width)


def solution(mesh):
    spec = P("seq", "head")
    return jax.shard_map(
        body, mesh=mesh, in_specs=(spec,) * 5 + (P("head"), P("seq", None)), out_specs=(spec,) * 4 + (P("head"),),
        check_vma=False,
    )
```

```python
import functools

import jax
import jax.numpy as jnp
from jax import lax
from jax.experimental import pallas as pl
from jax.experimental.pallas import tpu as pltpu
from jax.sharding import PartitionSpec as P

HD = 128
EPS = 1e-06
F32 = jnp.float32
BF16 = jnp.bfloat16
VMEM_LIMIT = 12 * 1024 * 1024
VMEM = pl.BlockSpec(memory_space=pltpu.VMEM)
SMEM = pl.BlockSpec(memory_space=pltpu.SMEM)
HBM = pl.BlockSpec(memory_space=pltpu.HBM)
ANY = pl.BlockSpec(memory_space=pl.ANY)
INTRA_SHARE = [1, 0, 2, 0, 1]
BACK_SHARE = [2, 3, 0, 1, 2]
BACK_SIZE = 1
LONG = 1 << 26


def dot(a, b, ca, cb):
    return lax.dot_general(a, b, (((ca,), (cb,)), ((), ())), preferred_element_type=F32)


def shape(dims, dtype=F32):
    return jax.ShapeDtypeStruct(dims, dtype)


def call(kernel, name, ins, outs, scratch=(), after=(), aliases=None, cost=1):
    after = list(after)

    def run(*refs):
        kernel(*refs[: len(ins)], *refs[len(ins) + len(after) :])

    return pl.pallas_call(
        run,
        name=name,
        out_shape=[o for o, _ in outs],
        in_specs=[s for _, s in ins] + [ANY] * len(after),
        out_specs=[s for _, s in outs],
        scratch_shapes=list(scratch),
        input_output_aliases=aliases or {},
        cost_estimate=pl.CostEstimate(flops=cost, bytes_accessed=cost, transcendentals=0),
        compiler_params=pltpu.CompilerParams(vmem_limit_bytes=VMEM_LIMIT),
    )(*[pltpu.with_memory_space_constraint(a, pltpu.HBM) if s is HBM else a for a, s in ins], *after)


def part(i, size):
    return slice(i * size, (i + 1) * size)


def shard_cols(chunk, quad, d, sw):
    member = lax.rem(lax.axis_index("seq"), quad)
    return pl.ds(pl.multiple_of((chunk * quad + (member ^ d)) * sw, sw), sw)


def sum_parts(parts):
    return functools.reduce(jnp.add, parts)


def head_at(chunk, quad, d, hs, h):
    member = lax.rem(lax.axis_index("seq"), quad)
    return pl.ds(pl.multiple_of(((chunk * quad + (member ^ d)) * hs + h) * HD, HD), HD)


def start_fetch(chunk, quad, base, steps, sw, pairs, sems):
    groups = []
    for d in range(steps):
        cols = shard_cols(chunk, quad, base + d, sw)
        group = [
            pltpu.make_async_copy(src.at[:, cols], dst.at[:, part(d, sw)], sems.at[i, d])
            for i, (src, dst) in enumerate(pairs)
        ]
        for copy in group:
            copy.start()
        groups.append(group)
    return groups


def write_masks(tiles, tile, mask, keep, keep_t):
    row = lax.broadcasted_iota(jnp.int32, (tile, tile), 0)
    col = lax.broadcasted_iota(jnp.int32, (tile, tile), 1)
    for i in range(tiles):
        for j in range(tiles):
            read = mask[i, j] == 1
            if i == j:
                keep[part(i, tile), part(j, tile)] = jnp.where(read & (row >= col), 1.0, 0.0).astype(BF16)
                keep_t[part(j, tile), part(i, tile)] = jnp.where(read & (row <= col), 1.0, 0.0).astype(BF16)
            else:
                value = jnp.where(read & (row >= 0), 1.0, 0.0).astype(BF16)
                keep[part(i, tile), part(j, tile)] = value
                keep_t[part(j, tile), part(i, tile)] = value


def states_kernel(quad, hs, chunk, tiles, tile, *refs):
    sw = hs * HD
    first = chunk == 0
    srcs, refs = refs[:2], refs[2:]
    if first:
        mask, refs = refs[0], refs[1:]
    (k_out, v_out), outs, refs = refs[:2], refs[2 : 2 + quad], refs[2 + quad :]
    if first:
        (keep, keep_t), refs = refs[:2], refs[2:]
    groups = start_fetch(chunk, quad, 0, quad, sw, list(zip(srcs, (k_out, v_out))), refs[0])
    if first:
        held, mask_sem = refs[-2:]
        copy = pltpu.make_async_copy(mask, held, mask_sem.at[0])
        copy.start()
        copy.wait()
        write_masks(tiles, tile, held, keep, keep_t)
    for d in range(quad):
        for copy in groups[d]:
            copy.wait()
        write_states(outs[d], k_out[:, part(d, sw)], v_out[:, part(d, sw)], hs)


def write_states(out, a, b, hs):
    if hs == 2:
        both = dot(a, b, 0, 0)
        for h in range(hs):
            out[part(h, HD), :] = both[part(h, HD), part(h, HD)]
    else:
        for h in range(hs):
            out[part(h, HD), :] = dot(a[:, part(h, HD)], b[:, part(h, HD)], 0, 0)


def intra_kernel(quad, hs, chunk, base, steps, blk, k, v, keep, q, gate, up, gain, intra, weight):
    rows = keep.shape[0]
    for d in range(steps):
        for h in range(hs):
            mine = part(d * hs + h, HD)
            cols = part((base + d) * hs + h, HD)
            at = head_at(chunk, quad, base + d, hs, h)
            outs = []
            for j in range(rows // blk):
                ks, after = part(j, blk), slice(j * blk, rows)
                probs = dot(q[after, at], k[ks, cols], 1, 1).astype(BF16) * keep[after, ks]
                outs.append(dot(probs, v[ks, cols], 1, 0))
            for i in range(rows // blk):
                intra[part(i, blk), mine] = sum_parts([outs[j][part(i - j, blk)] for j in range(i + 1)])
            sig = jax.nn.sigmoid(gate[:, at].astype(F32))
            weight[:, mine] = up[:, at].astype(F32) * sig * gain[:, at]


def packed_rows(j, blk):
    at = j * (j + 1) // 2 * blk
    return slice(at, at + (j + 1) * blk)


def probs_kernel(hs, quad, chunk, base, steps, blk, k, q, keep_t, probs):
    for d in range(steps):
        for h in range(hs):
            cols = part((base + d) * hs + h, HD)
            at = head_at(chunk, quad, base + d, hs, h)
            for j in range(keep_t.shape[0] // blk):
                qs, end = part(j, blk), (j + 1) * blk
                one = dot(k[:end, cols], q[qs, at], 1, 1).astype(BF16) * keep_t[:end, qs]
                probs[d * hs + h, packed_rows(j, blk), :] = one


def sums_kernel(hs, chunk, first, sides, pieces_n, q, *refs):
    intras, weights = refs[:sides], refs[sides : 2 * sides]
    pieces = refs[2 * sides : 2 * sides + pieces_n]
    rest = refs[2 * sides + pieces_n :]
    before, out, attn_out = (None, *rest) if first else rest
    steps = pieces_n // sides
    rows = q.shape[0]
    prefixes = [pieces[d][part(h, HD), :].astype(BF16) for d in range(pieces_n) for h in range(hs)]
    sums = []
    for r in range(0, rows, HD):
        here = slice(r, r + HD)
        squares = cross = None
        for d in range(pieces_n):
            side, at = d // steps, d % steps
            for h in range(hs):
                cols = part(at * hs + h, HD)
                cols_q = head_at(chunk, pieces_n, d, hs, h)
                attn = intras[side][here, cols] + dot(q[here, cols_q], prefixes[d * hs + h], 1, 0)
                attn_out[here, part(d * hs + h, HD)] = attn
                wide = weights[side][here, cols]
                squares = attn * attn if squares is None else squares + attn * attn
                cross = attn * wide if cross is None else cross + attn * wide
        sums.append([jnp.sum(one.T, 0, keepdims=True) for one in (squares, cross)])
    both = [jnp.concatenate([one[i] for one in sums], 1) for i in range(2)]
    total = jnp.concatenate(both + [jnp.zeros((6, rows), F32)], 0)
    out[...] = total if first else total + before[...]


def adjoint_kernel(hs, chunk, full, sides, quad, parts_n, carried, last, queries, attns, *refs):
    weights, refs = refs[:sides], refs[sides:]
    parts, refs = refs[:parts_n], refs[parts_n:]
    gains_before, refs = refs[:carried], refs[carried:]
    if chunk == 0:
        da, inverse, factor = refs[:3]
        outs = refs[3 : 3 + quad]
        total = parts[0][...]
        for one in parts[1:]:
            total = total + one[...]
        mean = total[0:1] * (1.0 / full) + EPS
        tall = (HD, total.shape[1])
        inverse[...] = jnp.broadcast_to(lax.rsqrt(mean), tall).T
        factor[...] = jnp.broadcast_to(total[1:2] * (1.0 / full) / mean, tall).T
    else:
        inverse, factor = parts
        da, outs = refs[0], refs[1 : 1 + quad]
    steps = quad // sides
    sw = hs * HD
    rows = queries.shape[0]
    block = 64 if rows % 64 == 0 else rows
    sums = [None] * (quad * hs)
    for r in range(0, rows, block):
        here = slice(r, r + block)
        scale, taken = inverse[here, :], factor[here, :]
        for i in range(quad * hs):
            side, at = i // (steps * hs), i % (steps * hs)
            attn, wide = attns[here, part(i, HD)], weights[side][here, part(at, HD)]
            da[here, part(i, HD)] = ((wide - attn * taken) * scale).astype(BF16)
            one = jnp.sum((wide * attn * scale).reshape(block // 8, 8, HD), 0)
            sums[i] = one if sums[i] is None else sums[i] + one
    gains = [jnp.sum(one, 0, keepdims=True) for one in sums]
    for d in range(quad):
        write_states(outs[d], queries[:, shard_cols(chunk, quad, d, sw)], da[:, part(d, sw)], hs)
        rows_out = gains[d * hs : (d + 1) * hs]
        if last:
            older = [g[part(d, hs), :] for g in gains_before]
            pad = outs[d].shape[0] - sw - (len(older) + 1) * hs
            zero = [jnp.zeros((pad, HD), F32)] if pad else []
            outs[d][sw:, :] = jnp.concatenate(older + rows_out + zero, 0)
        else:
            refs[-1][part(d, hs), :] = jnp.concatenate(rows_out, 0)


def total_kernel(sw, pieces_n, whole, *refs):
    total = refs[0][...]
    for one in refs[1:pieces_n]:
        total = total + one[...]
    refs[pieces_n][...] = total if whole else total[:sw]
    if len(refs) > pieces_n + 1:
        refs[pieces_n + 1][...] = total[sw:]


def give_kernel(sw, quad, later, smalls_n, gate_group, *refs):
    pieces, start, smalls, outs = refs[:quad], refs[quad], refs[quad + 1 : quad + 1 + smalls_n], refs[quad + 1 + smalls_n :]
    member = lax.rem(lax.axis_index("seq"), quad)
    values = [piece[:sw, :] for piece in pieces]
    begin = start[:sw, :]
    if gate_group is not None:
        begin = begin * jnp.where(lax.axis_index("seq") // quad == gate_group, 1.0, 0.0)
    for d in range(quad):
        total = begin
        for e in range(quad):
            if e != d:
                source, target = member ^ e, member ^ d
                take = source > target if later else source < target
                total = total + values[e] * jnp.where(take, 1.0, 0.0)
        outs[d][:sw, :] = total
    if smalls_n:
        small = outs[0].shape[0] - sw
        total = smalls[0][-small:, :]
        for one in smalls[1:]:
            total = total + one[...]
        if gate_group is not None:
            total = total + start[sw:, :]
        for d in range(quad):
            outs[d][sw:, :] = total


def back_kernel(hs, quad, chunk, base, at_side, steps, blk, k, v, da, keep, keep_t, q, gate, attns, weight, inverse, probs, *rest):
    pieces, (gq, ggate, gk, gv) = rest[:steps], rest[steps:]
    rows = keep.shape[0]
    n = rows // blk
    for d in range(steps):
        for h in range(hs):
            mine = part(d * hs + h, HD)
            cols = part((base + d) * hs + h, HD)
            at = head_at(chunk, quad, base + d, hs, h)
            in_side = (at_side + d) * hs + h
            prefix = pieces[d][part(h, HD), :].astype(BF16)
            linear = dot(da[:, cols], prefix, 1, 1)
            dprobs = [
                dot(da[j * blk :, cols], v[part(j, blk), cols], 1, 1).astype(BF16) * keep[j * blk :, part(j, blk)]
                for j in range(n)
            ]
            outs = [dot(dprobs[j], k[part(j, blk), cols], 1, 0) for j in range(n)]
            for i in range(n):
                pieces_q = [linear[part(i, blk)]] + [outs[j][part(i - j, blk)] for j in range(i + 1)]
                gq[part(i, blk), mine] = sum_parts(pieces_q).astype(BF16)
            outs_v, outs_k = [], []
            for j in range(n):
                qs, end = part(j, blk), (j + 1) * blk
                outs_v.append(dot(probs[in_side, packed_rows(j, blk), :], da[qs, cols], 1, 0))
                back = dot(v[:end, cols], da[qs, cols], 1, 1).astype(BF16) * keep_t[:end, qs]
                outs_k.append(dot(back, q[qs, at], 1, 0))
            for i in range(n):
                gv[part(i, blk), mine] = sum_parts([outs_v[j][part(i, blk)] for j in range(i, n)])
                gk[part(i, blk), mine] = sum_parts([outs_k[j][part(i, blk)] for j in range(i, n)])
            sig = jax.nn.sigmoid(gate[:, at].astype(F32))
            ggate[:, mine] = (weight[:, part(in_side, HD)] * attns[:, cols] * inverse[...] * (1.0 - sig)).astype(BF16)


def diagonals(piece, hs, at, d):
    sw = hs * HD
    if hs == 2:
        zero = jnp.zeros((HD, HD), BF16)
        one, two = piece[:HD, :].astype(BF16), piece[HD:sw, :].astype(BF16)
        both = jnp.concatenate([jnp.concatenate([one, zero], 1), jnp.concatenate([zero, two], 1)], 0)
        return [(part(at, sw), part(d, sw), both)]
    return [(part(at * hs + h, HD), part(d * hs + h, HD), piece[part(h, HD), :].astype(BF16)) for h in range(hs)]


def finish_kernel(hs, quad, chunk, chunks, sizes, olds, last, k, v, *rest):
    n = len(sizes)
    sw = hs * HD
    (gq_parts, ggate_parts, gk_parts, gv_parts), rest = [rest[i * n : (i + 1) * n] for i in range(4)], rest[4 * n :]
    pieces, rest = rest[:quad], rest[quad:]
    if last:
        gain, rest = rest[0], rest[1:]
    rest = rest[olds:]
    gq, ggate, gk, gv, rest = *rest[:4], rest[4:]
    if last:
        ggain, rest = rest[0], rest[1:]
    gk_out, gv_out, sems = rest
    copies = []
    where = [(i, at) for i, size in enumerate(sizes) for at in range(size)]

    def store(d, i, src, dst):
        copy = pltpu.make_async_copy(src, dst.at[:, shard_cols(chunk, quad, d, sw)], sems.at[i, d])
        copy.start()
        copies.append(copy)

    for d in range(quad):
        i, at = where[d]
        store(d, 0, gq_parts[i].at[:, part(at, sw)], gq)
        store(d, 1, ggate_parts[i].at[:, part(at, sw)], ggate)
    if last:
        for c in range(chunks):
            for d in range(quad):
                for h in range(hs):
                    at = head_at(c, quad, d, hs, h)
                    row = sw + c * hs + h
                    ggain[:, at] = pieces[d][row : row + 1, :] / gain[:, at]
    for d in range(quad):
        i, at = where[d]
        for mine, cols, suffix in diagonals(pieces[d], hs, at, d):
            gk_out[:, cols] = (gk_parts[i][:, mine] + dot(v[:, cols], suffix, 1, 1)).astype(BF16)
            gv_out[:, cols] = (gv_parts[i][:, mine] + dot(k[:, cols], suffix, 1, 0)).astype(BF16)
        store(d, 2, gk_out.at[:, part(d, sw)], gk)
        store(d, 3, gv_out.at[:, part(d, sw)], gv)
    for copy in copies:
        copy.wait()


def scatter(pieces, count):
    return [pieces[0]] + [
        lax.ppermute(pieces[d], "seq", [(b, b ^ d) for b in range(count)]) for d in range(1, len(pieces))
    ]


def carry(total, count, quad, later):
    groups = count // quad

    def shift(value, by):
        pairs = [(b, b + by * quad) for b in range(count - by * quad)]
        if later:
            pairs = [(t, s) for s, t in pairs]
        return lax.ppermute(value, "seq", pairs)

    if groups == 1:
        return jnp.zeros_like(total)
    total = shift(total, 1)
    by = 1
    while by < groups - 1:
        total = total + shift(total, by)
        by *= 2
    return total


def body(queries, keys, values, gate, grad_out, gain, tile_mask):
    rows, width = queries.shape
    heads = width // HD
    tiles = tile_mask.shape[0]
    tile = rows // tiles
    blk = 2 * tile if tiles % 2 == 0 else tile
    count, head_n = lax.axis_size("seq"), lax.axis_size("head")
    quad = next(g for g in (4, 2, 1) if count % g == 0 and heads % g == 0)
    chunks = 2 if heads % (2 * quad) == 0 else 1
    hs = heads // (quad * chunks)
    sw = hs * HD
    cw = quad * sw
    sides = 2 if quad % 2 == 0 else 1
    steps = quad // sides
    pw = steps * sw
    pad = -(-chunks * hs // 8) * 8
    every = range(chunks)
    final = chunks - 1
    gain_row = gain.reshape(1, width)
    full = float(width * head_n)
    dma = pltpu.SemaphoreType.DMA
    packed = (rows // blk) * (rows // blk + 1) // 2 * blk

    places = [(c, side) for c in every for side in range(sides)]

    def states(c, after):
        first = c == 0
        scratch = [dma((2, quad))]
        scratch += [pltpu.SMEM((tiles, tiles), jnp.int32), dma((1,))] if first else []
        return call(
            functools.partial(states_kernel, quad, hs, c, tiles, tile), "states",
            [(keys, HBM), (values, HBM)] + ([(tile_mask, HBM)] if first else []),
            [(shape((rows, cw), BF16), VMEM)] * 2 + [(shape((sw, HD)), VMEM)] * quad
            + ([(shape((rows, rows), BF16), VMEM)] * 2 if first else []),
            scratch, after,
        )

    def intra(c, side, k, v, after):
        return call(
            functools.partial(intra_kernel, quad, hs, c, side * steps, steps, blk), "intra",
            [(k, VMEM), (v, VMEM), (keep, VMEM), (queries, VMEM), (gate, VMEM), (grad_out, VMEM), (gain_row, VMEM)],
            [(shape((rows, pw)), VMEM)] * 2, [], after,
        )

    def token_sums(c, lots, prefix, before, after):
        extra = [] if before is None else [(before, VMEM)]
        return call(
            functools.partial(sums_kernel, hs, c, before is None, sides, quad), "token_sums",
            [(queries, VMEM)] + [(lot[i], VMEM) for i in (0, 1) for lot in lots] + [(p, VMEM) for p in prefix] + extra,
            [(shape((8, rows)), VMEM), (shape((rows, cw)), VMEM)], (), after, cost=LONG,
        )

    def adjoints(c, attn, parts, gains, after):
        last = c == final
        outs = [(shape((rows, cw), BF16), VMEM)] + ([(shape((rows, HD)), VMEM)] * 2 if c == 0 else [])
        outs += [(shape((sw + (pad if last else 0), HD)), VMEM)] * quad
        if not last:
            outs += [(shape((quad * hs, HD)), VMEM)]
        return call(
            functools.partial(adjoint_kernel, hs, c, full, sides, quad, len(parts), len(gains), last), "adjoints",
            [(queries, VMEM), (attn, VMEM)] + [(lot[1], VMEM) for lot in lots[c]] + [(p, VMEM) for p in parts]
            + [(g, VMEM) for g in gains],
            outs, [], after,
        )

    def probabilities(c, side, k, after):
        return call(
            functools.partial(probs_kernel, hs, quad, c, side * steps, steps, blk), "probs",
            [(k, VMEM), (queries, VMEM), (keep_t, VMEM)], [(shape((steps * hs, packed, blk), BF16), VMEM)], [], after,
        )[0]

    def totals(pieces, whole, after):
        size = pieces[0].shape[0]
        small = 0 if whole else size - sw
        return call(
            functools.partial(total_kernel, sw, quad, whole), "total", [(p, VMEM) for p in pieces],
            [(shape((size if whole else sw, HD)), VMEM)] + ([(shape((small, HD)), VMEM)] if small else []), (), after,
        )

    def give(pieces, start, smalls, later, gate_group, after):
        size = pieces[0].shape[0]
        return call(
            functools.partial(give_kernel, sw, quad, later, len(smalls), gate_group), "give",
            [(p, VMEM) for p in pieces] + [(start, VMEM)] + [(s, VMEM) for s in smalls],
            [(shape((size, HD)), VMEM)] * quad, (), after,
        )

    def back(c, base, size, k, v, da, inverse, prefix, after):
        side = base // steps
        ins = [(k, VMEM), (v, VMEM), (da, VMEM), (keep, VMEM), (keep_t, VMEM), (queries, VMEM), (gate, VMEM)]
        ins += [(attns[c], VMEM), (lots[c][side][1], VMEM), (inverse, VMEM), (probs[(c, side)], VMEM)]
        ins += [(p, VMEM) for p in prefix[base : base + size]]
        return call(
            functools.partial(back_kernel, hs, quad, c, base, base % steps, size, blk), "back", ins,
            [(shape((rows, size * sw), BF16), VMEM)] * 2 + [(shape((rows, size * sw)), VMEM)] * 2, [], after,
        )

    def finish(c, k, v, suffix, outs, after):
        last = c == final
        parts = halves[c]
        ins = [(k, VMEM), (v, VMEM)] + [(p[i], VMEM) for i in range(4) for p in parts] + [(s, VMEM) for s in suffix]
        ins += [(gain_row, VMEM)] if last else []
        aliases = {len(ins) + i: i for i in range(len(outs))}
        sizes = tuple(p[0].shape[1] // sw for p in parts)
        return call(
            functools.partial(finish_kernel, hs, quad, c, chunks, sizes, len(outs), last), "finish",
            ins + [(o, HBM) for o in outs],
            [(shape((rows, width), BF16), HBM)] * 4 + ([(shape((1, width)), VMEM)] if last else []),
            [pltpu.VMEM((rows, cw), BF16)] * 2 + [dma((4, quad))], after, aliases, cost=LONG,
        )

    def scan(messages, later, jobs):
        met = [scatter(m, count) for m in messages]
        done = messages[-1][:1]
        starts, smalls, gates = [], [[] for _ in every], [None for _ in every]
        pair = count == 2 * quad
        for c in every:
            done = jobs(c, done)
            total, *small = totals(met[c], pair, done)
            done = [total]
            if pair:
                starts.append(lax.ppermute(total, "seq", [(b, b ^ quad) for b in range(count)]))
                smalls[c] = [total] if total.shape[0] > sw else []
                gates[c] = 0 if later else 1
                continue
            starts.append(carry(total, count, quad, later))
            if small:
                smalls[c] = small + [
                    lax.ppermute(small[0], "seq", [(b, (b + s * quad) % count) for b in range(count)])
                    for s in range(1, count // quad)
                ]
        gives = []
        for c in every:
            done = jobs(chunks + c, done)
            out = give(met[c], starts[c], smalls[c], later, gates[c], done)
            done = out[:1]
            gives.append(scatter(out, count))
        return gives, jobs(2 * chunks, done)

    kv, messages, after = [], [], []
    for c in every:
        k, v, *pieces = states(c, after)
        if c == 0:
            keep, keep_t = pieces[quad : quad + 2]
        pieces = pieces[:quad]
        after = pieces[:1]
        kv.append((k, v))
        messages.append(pieces)
    lots = [[None] * sides for _ in every]
    def lots_of(items, share):
        cuts, total = [], 0
        for one in share:
            total += one
            cuts.append(round(total * len(items) / sum(share)))
        return [items[i:j] for i, j in zip([0] + cuts, cuts)]

    def windows(share):
        if chunks == 2:
            return share
        return [share[0] + share[1], share[2] + share[3], share[4]]

    intra_lots = lots_of(places, windows(INTRA_SHARE))

    def intra_jobs(window, after):
        for c, side in intra_lots[window]:
            lots[c][side] = intra(c, side, *kv[c], after)
            after = lots[c][side][:1]
        return after

    prefix, after = scan(messages, False, intra_jobs)
    sums, attns = None, []
    for c in every:
        sums, attn = token_sums(c, lots[c], prefix[c], sums, after)
        attns.append(attn)
        after = []
    parts = [sums] + [lax.ppermute(sums, "head", [(b, b ^ d) for b in range(head_n)]) for d in range(1, head_n)]
    after, probs = [sums], {}
    for place in places:
        probs[place] = probabilities(*place, kv[place[0]][0], after)
        after = [probs[place]]

    das, messages, gains = [], [], []
    for c in every:
        da, *pieces = adjoints(c, attns[c], parts if c == 0 else scales, gains if c == final else [], after)
        if c == 0:
            scales, pieces = pieces[:2], pieces[2:]
        after = []
        das.append(da)
        messages.append(pieces[:quad])
        gains += pieces[quad:]
    halves = [[] for _ in every]
    size = min(BACK_SIZE, steps)
    back_lots = lots_of([(c, d) for c in every for d in range(0, quad, size)], windows(BACK_SHARE))

    def back_jobs(window, after):
        for c, d in back_lots[window]:
            halves[c].append(back(c, d, size, *kv[c], das[c], scales[0], prefix[c], after))
            after = halves[c][-1][2:3]
        return after

    suffix, after = scan(messages, True, back_jobs)
    outs = []
    for c in every:
        outs = finish(c, *kv[c], suffix[c], outs[:4], after)
        after = []
    gq, ggate, gk, gv, ggain = outs
    return gq, gk, gv, ggate, ggain.reshape(width)


def solution(mesh):
    spec = P("seq", "head")
    return jax.shard_map(
        body, mesh=mesh, in_specs=(spec,) * 5 + (P("head"), P("seq", None)), out_specs=(spec,) * 4 + (P("head"),),
        check_vma=False,
    )
```

```python
import functools

import jax
import jax.numpy as jnp
from jax import lax
from jax.experimental import pallas as pl
from jax.experimental.pallas import tpu as pltpu
from jax.sharding import PartitionSpec as P

HD = 128
EPS = 1e-06
F32 = jnp.float32
BF16 = jnp.bfloat16
VMEM_LIMIT = 12 * 1024 * 1024
VMEM = pl.BlockSpec(memory_space=pltpu.VMEM)
SMEM = pl.BlockSpec(memory_space=pltpu.SMEM)
HBM = pl.BlockSpec(memory_space=pltpu.HBM)
ANY = pl.BlockSpec(memory_space=pl.ANY)
INTRA_SHARE = [1, 0, 2, 0, 1]
BACK_SHARE = [2, 3, 0, 1, 2]
JOIN = True
EARLY_PROBS = 1
LONG = 1 << 26


def dot(a, b, ca, cb):
    return lax.dot_general(a, b, (((ca,), (cb,)), ((), ())), preferred_element_type=F32)


def shape(dims, dtype=F32):
    return jax.ShapeDtypeStruct(dims, dtype)


def call(kernel, name, ins, outs, scratch=(), after=(), aliases=None, cost=1):
    after = list(after)

    def run(*refs):
        kernel(*refs[: len(ins)], *refs[len(ins) + len(after) :])

    return pl.pallas_call(
        run,
        name=name,
        out_shape=[o for o, _ in outs],
        in_specs=[s for _, s in ins] + [ANY] * len(after),
        out_specs=[s for _, s in outs],
        scratch_shapes=list(scratch),
        input_output_aliases=aliases or {},
        cost_estimate=pl.CostEstimate(flops=cost, bytes_accessed=cost, transcendentals=0),
        compiler_params=pltpu.CompilerParams(vmem_limit_bytes=VMEM_LIMIT),
    )(*[pltpu.with_memory_space_constraint(a, pltpu.HBM) if s is HBM else a for a, s in ins], *after)


def part(i, size):
    return slice(i * size, (i + 1) * size)


def shard_cols(chunk, quad, d, sw):
    member = lax.rem(lax.axis_index("seq"), quad)
    return pl.ds(pl.multiple_of((chunk * quad + (member ^ d)) * sw, sw), sw)


def sum_parts(parts):
    return functools.reduce(jnp.add, parts)


def head_at(chunk, quad, d, hs, h):
    member = lax.rem(lax.axis_index("seq"), quad)
    return pl.ds(pl.multiple_of(((chunk * quad + (member ^ d)) * hs + h) * HD, HD), HD)


def start_fetch(chunk, quad, base, steps, sw, pairs, sems):
    groups = []
    for d in range(steps):
        cols = shard_cols(chunk, quad, base + d, sw)
        group = [
            pltpu.make_async_copy(src.at[:, cols], dst.at[:, part(d, sw)], sems.at[i, d])
            for i, (src, dst) in enumerate(pairs)
        ]
        for copy in group:
            copy.start()
        groups.append(group)
    return groups


def write_masks(tiles, tile, mask, keep, keep_t):
    row = lax.broadcasted_iota(jnp.int32, (tile, tile), 0)
    col = lax.broadcasted_iota(jnp.int32, (tile, tile), 1)
    for i in range(tiles):
        for j in range(tiles):
            read = mask[i, j] == 1
            if i == j:
                keep[part(i, tile), part(j, tile)] = jnp.where(read & (row >= col), 1.0, 0.0).astype(BF16)
                keep_t[part(j, tile), part(i, tile)] = jnp.where(read & (row <= col), 1.0, 0.0).astype(BF16)
            else:
                value = jnp.where(read & (row >= 0), 1.0, 0.0).astype(BF16)
                keep[part(i, tile), part(j, tile)] = value
                keep_t[part(j, tile), part(i, tile)] = value


def states_kernel(quad, hs, chunk, tiles, tile, *refs):
    sw = hs * HD
    first = chunk == 0
    srcs, refs = refs[:2], refs[2:]
    if first:
        mask, refs = refs[0], refs[1:]
    (k_out, v_out), outs, refs = refs[:2], refs[2 : 2 + quad], refs[2 + quad :]
    if first:
        (keep, keep_t), refs = refs[:2], refs[2:]
    groups = start_fetch(chunk, quad, 0, quad, sw, list(zip(srcs, (k_out, v_out))), refs[0])
    if first:
        held, mask_sem = refs[-2:]
        copy = pltpu.make_async_copy(mask, held, mask_sem.at[0])
        copy.start()
        copy.wait()
        write_masks(tiles, tile, held, keep, keep_t)
    for d in range(quad):
        for copy in groups[d]:
            copy.wait()
        write_states(outs[d], k_out[:, part(d, sw)], v_out[:, part(d, sw)], hs)


def write_states(out, a, b, hs):
    if hs == 2:
        both = dot(a, b, 0, 0)
        for h in range(hs):
            out[part(h, HD), :] = both[part(h, HD), part(h, HD)]
    else:
        for h in range(hs):
            out[part(h, HD), :] = dot(a[:, part(h, HD)], b[:, part(h, HD)], 0, 0)


def intra_kernel(quad, hs, chunk, base, steps, blk, k, v, keep, q, gate, up, gain, intra, weight):
    rows = keep.shape[0]
    for d in range(steps):
        for h in range(hs):
            mine = part(d * hs + h, HD)
            cols = part((base + d) * hs + h, HD)
            at = head_at(chunk, quad, base + d, hs, h)
            outs = []
            for j in range(rows // blk):
                ks, after = part(j, blk), slice(j * blk, rows)
                probs = dot(q[after, at], k[ks, cols], 1, 1).astype(BF16) * keep[after, ks]
                outs.append(dot(probs, v[ks, cols], 1, 0))
            for i in range(rows // blk):
                intra[part(i, blk), mine] = sum_parts([outs[j][part(i - j, blk)] for j in range(i + 1)])
            sig = jax.nn.sigmoid(gate[:, at].astype(F32))
            weight[:, mine] = up[:, at].astype(F32) * sig * gain[:, at]


def packed_rows(j, blk):
    at = j * (j + 1) // 2 * blk
    return slice(at, at + (j + 1) * blk)


def probs_kernel(hs, quad, chunk, base, steps, blk, k, q, keep_t, probs):
    for d in range(steps):
        for h in range(hs):
            cols = part((base + d) * hs + h, HD)
            at = head_at(chunk, quad, base + d, hs, h)
            for j in range(keep_t.shape[0] // blk):
                qs, end = part(j, blk), (j + 1) * blk
                one = dot(k[:end, cols], q[qs, at], 1, 1).astype(BF16) * keep_t[:end, qs]
                probs[d * hs + h, packed_rows(j, blk), :] = one


def sums_kernel(hs, chunk, first, sides, pieces_n, q, *refs):
    intras, weights = refs[:sides], refs[sides : 2 * sides]
    pieces = refs[2 * sides : 2 * sides + pieces_n]
    rest = refs[2 * sides + pieces_n :]
    before, out, attn_out = (None, *rest) if first else rest
    steps = pieces_n // sides
    rows = q.shape[0]
    prefixes = [pieces[d][part(h, HD), :].astype(BF16) for d in range(pieces_n) for h in range(hs)]
    sums = []
    for r in range(0, rows, HD):
        here = slice(r, r + HD)
        squares = cross = None
        for d in range(pieces_n):
            side, at = d // steps, d % steps
            for h in range(hs):
                cols = part(at * hs + h, HD)
                cols_q = head_at(chunk, pieces_n, d, hs, h)
                attn = intras[side][here, cols] + dot(q[here, cols_q], prefixes[d * hs + h], 1, 0)
                attn_out[here, part(d * hs + h, HD)] = attn
                wide = weights[side][here, cols]
                squares = attn * attn if squares is None else squares + attn * attn
                cross = attn * wide if cross is None else cross + attn * wide
        sums.append([jnp.sum(one.T, 0, keepdims=True) for one in (squares, cross)])
    both = [jnp.concatenate([one[i] for one in sums], 1) for i in range(2)]
    total = jnp.concatenate(both + [jnp.zeros((6, rows), F32)], 0)
    out[...] = total if first else total + before[...]


def adjoint_kernel(hs, chunk, full, sides, quad, parts_n, carried, last, queries, attns, *refs):
    weights, refs = refs[:sides], refs[sides:]
    parts, refs = refs[:parts_n], refs[parts_n:]
    gains_before, refs = refs[:carried], refs[carried:]
    if chunk == 0:
        da, inverse, factor = refs[:3]
        outs = refs[3 : 3 + quad]
        total = parts[0][...]
        for one in parts[1:]:
            total = total + one[...]
        mean = total[0:1] * (1.0 / full) + EPS
        tall = (HD, total.shape[1])
        inverse[...] = jnp.broadcast_to(lax.rsqrt(mean), tall).T
        factor[...] = jnp.broadcast_to(total[1:2] * (1.0 / full) / mean, tall).T
    else:
        inverse, factor = parts
        da, outs = refs[0], refs[1 : 1 + quad]
    steps = quad // sides
    sw = hs * HD
    rows = queries.shape[0]
    block = 64 if rows % 64 == 0 else rows
    sums = [None] * (quad * hs)
    for r in range(0, rows, block):
        here = slice(r, r + block)
        scale, taken = inverse[here, :], factor[here, :]
        for i in range(quad * hs):
            side, at = i // (steps * hs), i % (steps * hs)
            attn, wide = attns[here, part(i, HD)], weights[side][here, part(at, HD)]
            da[here, part(i, HD)] = ((wide - attn * taken) * scale).astype(BF16)
            one = jnp.sum((wide * attn * scale).reshape(block // 8, 8, HD), 0)
            sums[i] = one if sums[i] is None else sums[i] + one
    gains = [jnp.sum(one, 0, keepdims=True) for one in sums]
    for d in range(quad):
        write_states(outs[d], queries[:, shard_cols(chunk, quad, d, sw)], da[:, part(d, sw)], hs)
        rows_out = gains[d * hs : (d + 1) * hs]
        if last:
            older = [g[part(d, hs), :] for g in gains_before]
            pad = outs[d].shape[0] - sw - (len(older) + 1) * hs
            zero = [jnp.zeros((pad, HD), F32)] if pad else []
            outs[d][sw:, :] = jnp.concatenate(older + rows_out + zero, 0)
        else:
            refs[-1][part(d, hs), :] = jnp.concatenate(rows_out, 0)


def total_kernel(sw, pieces_n, whole, *refs):
    total = refs[0][...]
    for one in refs[1:pieces_n]:
        total = total + one[...]
    refs[pieces_n][...] = total if whole else total[:sw]
    if len(refs) > pieces_n + 1:
        refs[pieces_n + 1][...] = total[sw:]


def give_kernel(sw, quad, later, smalls_n, gate_group, *refs):
    pieces, start, smalls, outs = refs[:quad], refs[quad], refs[quad + 1 : quad + 1 + smalls_n], refs[quad + 1 + smalls_n :]
    member = lax.rem(lax.axis_index("seq"), quad)
    values = [piece[:sw, :] for piece in pieces]
    begin = start[:sw, :]
    if gate_group is not None:
        begin = begin * jnp.where(lax.axis_index("seq") // quad == gate_group, 1.0, 0.0)
    for d in range(quad):
        total = begin
        for e in range(quad):
            if e != d:
                source, target = member ^ e, member ^ d
                take = source > target if later else source < target
                total = total + values[e] * jnp.where(take, 1.0, 0.0)
        outs[d][:sw, :] = total
    if smalls_n:
        small = outs[0].shape[0] - sw
        total = smalls[0][-small:, :]
        for one in smalls[1:]:
            total = total + one[...]
        if gate_group is not None:
            total = total + start[sw:, :]
        for d in range(quad):
            outs[d][sw:, :] = total


def back_kernel(hs, quad, chunk, base, at_side, steps, blk, k, v, da, keep, keep_t, q, gate, attns, weight, inverse, probs, *rest):
    pieces, (gq, ggate, gk, gv) = rest[:steps], rest[steps:]
    rows = keep.shape[0]
    n = rows // blk
    for d in range(steps):
        for h in range(hs):
            mine = part(d * hs + h, HD)
            cols = part((base + d) * hs + h, HD)
            at = head_at(chunk, quad, base + d, hs, h)
            in_side = (at_side + d) * hs + h
            prefix = pieces[d][part(h, HD), :].astype(BF16)
            linear = dot(da[:, cols], prefix, 1, 1)
            dprobs = [
                dot(da[j * blk :, cols], v[part(j, blk), cols], 1, 1).astype(BF16) * keep[j * blk :, part(j, blk)]
                for j in range(n)
            ]
            outs = [dot(dprobs[j], k[part(j, blk), cols], 1, 0) for j in range(n)]
            for i in range(n):
                pieces_q = [linear[part(i, blk)]] + [outs[j][part(i - j, blk)] for j in range(i + 1)]
                gq[part(i, blk), mine] = sum_parts(pieces_q).astype(BF16)
            outs_v, outs_k = [], []
            for j in range(n):
                qs, end = part(j, blk), (j + 1) * blk
                outs_v.append(dot(probs[in_side, packed_rows(j, blk), :], da[qs, cols], 1, 0))
                back = dot(v[:end, cols], da[qs, cols], 1, 1).astype(BF16) * keep_t[:end, qs]
                outs_k.append(dot(back, q[qs, at], 1, 0))
            for i in range(n):
                gv[part(i, blk), mine] = sum_parts([outs_v[j][part(i, blk)] for j in range(i, n)])
                gk[part(i, blk), mine] = sum_parts([outs_k[j][part(i, blk)] for j in range(i, n)])
            sig = jax.nn.sigmoid(gate[:, at].astype(F32))
            ggate[:, mine] = (weight[:, part(in_side, HD)] * attns[:, cols] * inverse[...] * (1.0 - sig)).astype(BF16)


def diagonals(piece, hs, at, d):
    sw = hs * HD
    if hs == 2:
        zero = jnp.zeros((HD, HD), BF16)
        one, two = piece[:HD, :].astype(BF16), piece[HD:sw, :].astype(BF16)
        both = jnp.concatenate([jnp.concatenate([one, zero], 1), jnp.concatenate([zero, two], 1)], 0)
        return [(part(at, sw), part(d, sw), both)]
    return [(part(at * hs + h, HD), part(d * hs + h, HD), piece[part(h, HD), :].astype(BF16)) for h in range(hs)]


def finish_kernel(hs, quad, chunk, chunks, sizes, olds, last, k, v, *rest):
    n = len(sizes)
    sw = hs * HD
    (gq_parts, ggate_parts, gk_parts, gv_parts), rest = [rest[i * n : (i + 1) * n] for i in range(4)], rest[4 * n :]
    pieces, rest = rest[:quad], rest[quad:]
    if last:
        gain, rest = rest[0], rest[1:]
    rest = rest[olds:]
    gq, ggate, gk, gv, rest = *rest[:4], rest[4:]
    if last:
        ggain, rest = rest[0], rest[1:]
    gk_out, gv_out, sems, *rest = rest
    copies = []
    where = [(i, at) for i, size in enumerate(sizes) for at in range(size)]

    def store(d, i, src, dst):
        copy = pltpu.make_async_copy(src, dst.at[:, shard_cols(chunk, quad, d, sw)], sems.at[i, d])
        copy.start()
        copies.append(copy)

    for d in range(quad):
        i, at = where[d]
        store(d, 0, gq_parts[i].at[:, part(at, sw)], gq)
        store(d, 1, ggate_parts[i].at[:, part(at, sw)], ggate)
    if last:
        ggain_out, ggain_sem = rest
        for c in range(chunks):
            for d in range(quad):
                for h in range(hs):
                    at = head_at(c, quad, d, hs, h)
                    row = sw + c * hs + h
                    ggain_out[:, at] = pieces[d][row : row + 1, :] / gain[:, at]
        copy = pltpu.make_async_copy(ggain_out, ggain, ggain_sem.at[0])
        copy.start()
        copies.append(copy)
    for d in range(quad):
        i, at = where[d]
        for mine, cols, suffix in diagonals(pieces[d], hs, at, d):
            gk_out[:, cols] = (gk_parts[i][:, mine] + dot(v[:, cols], suffix, 1, 1)).astype(BF16)
            gv_out[:, cols] = (gv_parts[i][:, mine] + dot(k[:, cols], suffix, 1, 0)).astype(BF16)
        store(d, 2, gk_out.at[:, part(d, sw)], gk)
        store(d, 3, gv_out.at[:, part(d, sw)], gv)
    for copy in copies:
        copy.wait()


def scatter(pieces, count):
    return [pieces[0]] + [
        lax.ppermute(pieces[d], "seq", [(b, b ^ d) for b in range(count)]) for d in range(1, len(pieces))
    ]


def carry(total, count, quad, later):
    groups = count // quad

    def shift(value, by):
        pairs = [(b, b + by * quad) for b in range(count - by * quad)]
        if later:
            pairs = [(t, s) for s, t in pairs]
        return lax.ppermute(value, "seq", pairs)

    if groups == 1:
        return jnp.zeros_like(total)
    total = shift(total, 1)
    by = 1
    while by < groups - 1:
        total = total + shift(total, by)
        by *= 2
    return total


def body(queries, keys, values, gate, grad_out, gain, tile_mask):
    rows, width = queries.shape
    heads = width // HD
    tiles = tile_mask.shape[0]
    tile = rows // tiles
    blk = 2 * tile if tiles % 2 == 0 else tile
    count, head_n = lax.axis_size("seq"), lax.axis_size("head")
    quad = next(g for g in (4, 2, 1) if count % g == 0 and heads % g == 0)
    chunks = 2 if heads % (2 * quad) == 0 else 1
    hs = heads // (quad * chunks)
    sw = hs * HD
    cw = quad * sw
    sides = 2 if quad % 2 == 0 else 1
    steps = quad // sides
    pw = steps * sw
    pad = -(-chunks * hs // 8) * 8
    every = range(chunks)
    final = chunks - 1
    gain_row = gain.reshape(1, width)
    full = float(width * head_n)
    dma = pltpu.SemaphoreType.DMA
    packed = (rows // blk) * (rows // blk + 1) // 2 * blk

    places = [(c, side) for c in every for side in range(sides)]

    def states(c, after):
        first = c == 0
        scratch = [dma((2, quad))]
        scratch += [pltpu.SMEM((tiles, tiles), jnp.int32), dma((1,))] if first else []
        return call(
            functools.partial(states_kernel, quad, hs, c, tiles, tile), "states",
            [(keys, HBM), (values, HBM)] + ([(tile_mask, HBM)] if first else []),
            [(shape((rows, cw), BF16), VMEM)] * 2 + [(shape((sw, HD)), VMEM)] * quad
            + ([(shape((rows, rows), BF16), VMEM)] * 2 if first else []),
            scratch, after,
        )

    def intra(c, side, k, v, after):
        return call(
            functools.partial(intra_kernel, quad, hs, c, side * steps, steps, blk), "intra",
            [(k, VMEM), (v, VMEM), (keep, VMEM), (queries, VMEM), (gate, VMEM), (grad_out, VMEM), (gain_row, VMEM)],
            [(shape((rows, pw)), VMEM)] * 2, [], after,
        )

    def token_sums(c, lots, prefix, before, after):
        extra = [] if before is None else [(before, VMEM)]
        return call(
            functools.partial(sums_kernel, hs, c, before is None, sides, quad), "token_sums",
            [(queries, VMEM)] + [(lot[i], VMEM) for i in (0, 1) for lot in lots] + [(p, VMEM) for p in prefix] + extra,
            [(shape((8, rows)), VMEM), (shape((rows, cw)), VMEM)], (), after, cost=LONG,
        )

    def adjoints(c, attn, parts, gains, after):
        last = c == final
        outs = [(shape((rows, cw), BF16), VMEM)] + ([(shape((rows, HD)), VMEM)] * 2 if c == 0 else [])
        outs += [(shape((sw + (pad if last else 0), HD)), VMEM)] * quad
        if not last:
            outs += [(shape((quad * hs, HD)), VMEM)]
        return call(
            functools.partial(adjoint_kernel, hs, c, full, sides, quad, len(parts), len(gains), last), "adjoints",
            [(queries, VMEM), (attn, VMEM)] + [(lot[1], VMEM) for lot in lots[c]] + [(p, VMEM) for p in parts]
            + [(g, VMEM) for g in gains],
            outs, [], after,
        )

    def probabilities(c, side, k, after):
        return call(
            functools.partial(probs_kernel, hs, quad, c, side * steps, steps, blk), "probs",
            [(k, VMEM), (queries, VMEM), (keep_t, VMEM)], [(shape((steps * hs, packed, blk), BF16), VMEM)], [], after,
        )[0]

    def totals(pieces, whole, after):
        size = pieces[0].shape[0]
        small = 0 if whole else size - sw
        return call(
            functools.partial(total_kernel, sw, quad, whole), "total", [(p, VMEM) for p in pieces],
            [(shape((size if whole else sw, HD)), VMEM)] + ([(shape((small, HD)), VMEM)] if small else []), (), after,
        )

    def give(pieces, start, smalls, later, gate_group, after):
        size = pieces[0].shape[0]
        return call(
            functools.partial(give_kernel, sw, quad, later, len(smalls), gate_group), "give",
            [(p, VMEM) for p in pieces] + [(start, VMEM)] + [(s, VMEM) for s in smalls],
            [(shape((size, HD)), VMEM)] * quad, (), after,
        )

    def back(c, base, size, k, v, da, inverse, prefix, after):
        side = base // steps
        ins = [(k, VMEM), (v, VMEM), (da, VMEM), (keep, VMEM), (keep_t, VMEM), (queries, VMEM), (gate, VMEM)]
        ins += [(attns[c], VMEM), (lots[c][side][1], VMEM), (inverse, VMEM), (probs[(c, side)], VMEM)]
        ins += [(p, VMEM) for p in prefix[base : base + size]]
        return call(
            functools.partial(back_kernel, hs, quad, c, base, base % steps, size, blk), "back", ins,
            [(shape((rows, size * sw), BF16), VMEM)] * 2 + [(shape((rows, size * sw)), VMEM)] * 2, [], after,
        )

    def finish(c, k, v, suffix, outs, after):
        last = c == final
        parts = halves[c]
        ins = [(k, VMEM), (v, VMEM)] + [(p[i], VMEM) for i in range(4) for p in parts] + [(s, VMEM) for s in suffix]
        ins += [(gain_row, VMEM)] if last else []
        aliases = {len(ins) + i: i for i in range(len(outs))}
        sizes = tuple(p[0].shape[1] // sw for p in parts)
        return call(
            functools.partial(finish_kernel, hs, quad, c, chunks, sizes, len(outs), last), "finish",
            ins + [(o, HBM) for o in outs],
            [(shape((rows, width), BF16), HBM)] * 4 + ([(shape((1, width)), HBM)] if last else []),
            [pltpu.VMEM((rows, cw), BF16)] * 2 + [dma((4, quad))]
            + ([pltpu.VMEM((1, width), F32), dma((1,))] if last else []), after, aliases, cost=LONG,
        )

    def scan(messages, later, jobs):
        met = [scatter(m, count) for m in messages]
        done = messages[-1][:1]
        starts, smalls, gates = [], [[] for _ in every], [None for _ in every]
        pair = count == 2 * quad
        for c in every:
            done = jobs(c, done)
            total, *small = totals(met[c], pair, done)
            done = [total]
            if pair:
                starts.append(lax.ppermute(total, "seq", [(b, b ^ quad) for b in range(count)]))
                smalls[c] = [total] if total.shape[0] > sw else []
                gates[c] = 0 if later else 1
                continue
            starts.append(carry(total, count, quad, later))
            if small:
                smalls[c] = small + [
                    lax.ppermute(small[0], "seq", [(b, (b + s * quad) % count) for b in range(count)])
                    for s in range(1, count // quad)
                ]
        gives = []
        for c in every:
            done = jobs(chunks + c, done)
            out = give(met[c], starts[c], smalls[c], later, gates[c], done)
            done = out[:1]
            gives.append(scatter(out, count))
        return gives, jobs(2 * chunks, done)

    kv, messages, after = [], [], []
    for c in every:
        k, v, *pieces = states(c, after)
        if c == 0:
            keep, keep_t = pieces[quad : quad + 2]
        pieces = pieces[:quad]
        after = pieces[:1]
        kv.append((k, v))
        messages.append(pieces)
    lots = [[None] * sides for _ in every]
    def lots_of(items, share):
        cuts, total = [], 0
        for one in share:
            total += one
            cuts.append(round(total * len(items) / sum(share)))
        return [items[i:j] for i, j in zip([0] + cuts, cuts)]

    def windows(share):
        if chunks == 2:
            return share
        return [share[0] + share[1], share[2] + share[3], share[4]]

    intra_lots = lots_of(places, windows(INTRA_SHARE))

    def intra_jobs(window, after):
        for c, side in intra_lots[window]:
            lots[c][side] = intra(c, side, *kv[c], after)
            after = lots[c][side][:1]
        return after

    prefix, after = scan(messages, False, intra_jobs)
    sums, attns, probs = None, [], {}

    def all_probs(picked, after):
        for place in picked:
            probs[place] = probabilities(*place, kv[place[0]][0], after)
            after = [probs[place]]
        return after

    for c in every:
        sums, attn = token_sums(c, lots[c], prefix[c], sums, after)
        attns.append(attn)
        after = all_probs(places[:EARLY_PROBS], [attn]) if c == final - 1 else []
    parts = [sums] + [lax.ppermute(sums, "head", [(b, b ^ d) for b in range(head_n)]) for d in range(1, head_n)]
    after = all_probs([place for place in places if place not in probs], [sums])

    das, messages, gains = [], [], []
    for c in every:
        da, *pieces = adjoints(c, attns[c], parts if c == 0 else scales, gains if c == final else [], after)
        if c == 0:
            scales, pieces = pieces[:2], pieces[2:]
        after = []
        das.append(da)
        messages.append(pieces[:quad])
        gains += pieces[quad:]
    halves = [[] for _ in every]
    back_lots = lots_of([(c, d) for c in every for d in range(quad)], windows(BACK_SHARE))

    def joined(lot):
        out = []
        for c, d in lot:
            if JOIN and out and d % steps and out[-1][0] == c and out[-1][1] + out[-1][2] == d:
                out[-1] = (c, out[-1][1], out[-1][2] + 1)
            else:
                out.append((c, d, 1))
        return out

    def back_jobs(window, after):
        for c, d, size in joined(back_lots[window]):
            halves[c].append(back(c, d, size, *kv[c], das[c], scales[0], prefix[c], after))
            after = halves[c][-1][2:3]
        return after

    suffix, after = scan(messages, True, back_jobs)
    outs = []
    for c in every:
        outs = finish(c, *kv[c], suffix[c], outs[:4], after)
        after = []
    gq, ggate, gk, gv, ggain = outs
    return gq, gk, gv, ggate, ggain.reshape(width)


def solution(mesh):
    spec = P("seq", "head")
    return jax.shard_map(
        body, mesh=mesh, in_specs=(spec,) * 5 + (P("head"), P("seq", None)), out_specs=(spec,) * 4 + (P("head"),),
        check_vma=False,
    )
```

```python
import functools

import jax
import jax.numpy as jnp
from jax import lax
from jax.experimental import pallas as pl
from jax.experimental.pallas import tpu as pltpu
from jax.sharding import PartitionSpec as P

HD = 128
EPS = 1e-06
F32 = jnp.float32
BF16 = jnp.bfloat16
VMEM_LIMIT = 12 * 1024 * 1024
VMEM = pl.BlockSpec(memory_space=pltpu.VMEM)
SMEM = pl.BlockSpec(memory_space=pltpu.SMEM)
HBM = pl.BlockSpec(memory_space=pltpu.HBM)
ANY = pl.BlockSpec(memory_space=pl.ANY)
INTRA_SHARE = [1, 1, 1, 0, 1]
BACK_SHARE = [2, 3, 0, 2, 1]
JOIN = True
EARLY_PROBS = 1
LONG = 1 << 26


def dot(a, b, ca, cb):
    return lax.dot_general(a, b, (((ca,), (cb,)), ((), ())), preferred_element_type=F32)


def shape(dims, dtype=F32):
    return jax.ShapeDtypeStruct(dims, dtype)


def call(kernel, name, ins, outs, scratch=(), after=(), aliases=None, cost=1):
    after = list(after)

    def run(*refs):
        kernel(*refs[: len(ins)], *refs[len(ins) + len(after) :])

    return pl.pallas_call(
        run,
        name=name,
        out_shape=[o for o, _ in outs],
        in_specs=[s for _, s in ins] + [ANY] * len(after),
        out_specs=[s for _, s in outs],
        scratch_shapes=list(scratch),
        input_output_aliases=aliases or {},
        cost_estimate=pl.CostEstimate(flops=cost, bytes_accessed=cost, transcendentals=0),
        compiler_params=pltpu.CompilerParams(vmem_limit_bytes=VMEM_LIMIT),
    )(*[pltpu.with_memory_space_constraint(a, pltpu.HBM) if s is HBM else a for a, s in ins], *after)


def part(i, size):
    return slice(i * size, (i + 1) * size)


def shard_cols(chunk, quad, d, sw):
    member = lax.rem(lax.axis_index("seq"), quad)
    return pl.ds(pl.multiple_of((chunk * quad + (member ^ d)) * sw, sw), sw)


def sum_parts(parts):
    return functools.reduce(jnp.add, parts)


def head_at(chunk, quad, d, hs, h):
    member = lax.rem(lax.axis_index("seq"), quad)
    return pl.ds(pl.multiple_of(((chunk * quad + (member ^ d)) * hs + h) * HD, HD), HD)


def start_fetch(chunk, quad, base, steps, sw, pairs, sems):
    groups = []
    for d in range(steps):
        cols = shard_cols(chunk, quad, base + d, sw)
        group = [
            pltpu.make_async_copy(src.at[:, cols], dst.at[:, part(d, sw)], sems.at[i, d])
            for i, (src, dst) in enumerate(pairs)
        ]
        for copy in group:
            copy.start()
        groups.append(group)
    return groups


def write_masks(tiles, tile, mask, keep, keep_t):
    row = lax.broadcasted_iota(jnp.int32, (tile, tile), 0)
    col = lax.broadcasted_iota(jnp.int32, (tile, tile), 1)
    for i in range(tiles):
        for j in range(tiles):
            read = mask[i, j] == 1
            if i == j:
                keep[part(i, tile), part(j, tile)] = jnp.where(read & (row >= col), 1.0, 0.0).astype(BF16)
                keep_t[part(j, tile), part(i, tile)] = jnp.where(read & (row <= col), 1.0, 0.0).astype(BF16)
            else:
                value = jnp.where(read & (row >= 0), 1.0, 0.0).astype(BF16)
                keep[part(i, tile), part(j, tile)] = value
                keep_t[part(j, tile), part(i, tile)] = value


def states_kernel(quad, hs, chunk, tiles, tile, *refs):
    sw = hs * HD
    first = chunk == 0
    srcs, refs = refs[:2], refs[2:]
    if first:
        mask, refs = refs[0], refs[1:]
    (k_out, v_out), outs, refs = refs[:2], refs[2 : 2 + quad], refs[2 + quad :]
    if first:
        (keep, keep_t), refs = refs[:2], refs[2:]
    groups = start_fetch(chunk, quad, 0, quad, sw, list(zip(srcs, (k_out, v_out))), refs[0])
    if first:
        held, mask_sem = refs[-2:]
        copy = pltpu.make_async_copy(mask, held, mask_sem.at[0])
        copy.start()
        copy.wait()
        write_masks(tiles, tile, held, keep, keep_t)
    for d in range(quad):
        for copy in groups[d]:
            copy.wait()
        write_states(outs[d], k_out[:, part(d, sw)], v_out[:, part(d, sw)], hs)


def write_states(out, a, b, hs):
    if hs == 2:
        both = dot(a, b, 0, 0)
        for h in range(hs):
            out[part(h, HD), :] = both[part(h, HD), part(h, HD)]
    else:
        for h in range(hs):
            out[part(h, HD), :] = dot(a[:, part(h, HD)], b[:, part(h, HD)], 0, 0)


def intra_kernel(quad, hs, chunk, base, steps, blk, k, v, keep, q, gate, up, gain, intra, weight):
    rows = keep.shape[0]
    for d in range(steps):
        for h in range(hs):
            mine = part(d * hs + h, HD)
            cols = part((base + d) * hs + h, HD)
            at = head_at(chunk, quad, base + d, hs, h)
            outs = []
            for j in range(rows // blk):
                ks, after = part(j, blk), slice(j * blk, rows)
                probs = dot(q[after, at], k[ks, cols], 1, 1).astype(BF16) * keep[after, ks]
                outs.append(dot(probs, v[ks, cols], 1, 0))
            for i in range(rows // blk):
                intra[part(i, blk), mine] = sum_parts([outs[j][part(i - j, blk)] for j in range(i + 1)])
            sig = jax.nn.sigmoid(gate[:, at].astype(F32))
            weight[:, mine] = up[:, at].astype(F32) * sig * gain[:, at]


def packed_rows(j, blk):
    at = j * (j + 1) // 2 * blk
    return slice(at, at + (j + 1) * blk)


def probs_kernel(hs, quad, chunk, base, steps, blk, k, q, keep_t, probs):
    for d in range(steps):
        for h in range(hs):
            cols = part((base + d) * hs + h, HD)
            at = head_at(chunk, quad, base + d, hs, h)
            for j in range(keep_t.shape[0] // blk):
                qs, end = part(j, blk), (j + 1) * blk
                one = dot(k[:end, cols], q[qs, at], 1, 1).astype(BF16) * keep_t[:end, qs]
                probs[d * hs + h, packed_rows(j, blk), :] = one


def sums_kernel(hs, chunk, first, sides, pieces_n, q, *refs):
    intras, weights = refs[:sides], refs[sides : 2 * sides]
    pieces = refs[2 * sides : 2 * sides + pieces_n]
    rest = refs[2 * sides + pieces_n :]
    before, out, attn_out = (None, *rest) if first else rest
    steps = pieces_n // sides
    rows = q.shape[0]
    prefixes = [pieces[d][part(h, HD), :].astype(BF16) for d in range(pieces_n) for h in range(hs)]
    sums = []
    for r in range(0, rows, HD):
        here = slice(r, r + HD)
        squares = cross = None
        for d in range(pieces_n):
            side, at = d // steps, d % steps
            for h in range(hs):
                cols = part(at * hs + h, HD)
                cols_q = head_at(chunk, pieces_n, d, hs, h)
                attn = intras[side][here, cols] + dot(q[here, cols_q], prefixes[d * hs + h], 1, 0)
                attn_out[here, part(d * hs + h, HD)] = attn
                wide = weights[side][here, cols]
                squares = attn * attn if squares is None else squares + attn * attn
                cross = attn * wide if cross is None else cross + attn * wide
        sums.append([jnp.sum(one.T, 0, keepdims=True) for one in (squares, cross)])
    both = [jnp.concatenate([one[i] for one in sums], 1) for i in range(2)]
    total = jnp.concatenate(both + [jnp.zeros((6, rows), F32)], 0)
    out[...] = total if first else total + before[...]


def adjoint_kernel(hs, chunk, full, sides, quad, parts_n, carried, last, queries, attns, *refs):
    weights, refs = refs[:sides], refs[sides:]
    parts, refs = refs[:parts_n], refs[parts_n:]
    gains_before, refs = refs[:carried], refs[carried:]
    if chunk == 0:
        da, inverse, factor = refs[:3]
        outs = refs[3 : 3 + quad]
        total = parts[0][...]
        for one in parts[1:]:
            total = total + one[...]
        mean = total[0:1] * (1.0 / full) + EPS
        tall = (HD, total.shape[1])
        inverse[...] = jnp.broadcast_to(lax.rsqrt(mean), tall).T
        factor[...] = jnp.broadcast_to(total[1:2] * (1.0 / full) / mean, tall).T
    else:
        inverse, factor = parts
        da, outs = refs[0], refs[1 : 1 + quad]
    steps = quad // sides
    sw = hs * HD
    rows = queries.shape[0]
    block = 64 if rows % 64 == 0 else rows
    sums = [None] * (quad * hs)
    for r in range(0, rows, block):
        here = slice(r, r + block)
        scale, taken = inverse[here, :], factor[here, :]
        for i in range(quad * hs):
            side, at = i // (steps * hs), i % (steps * hs)
            attn, wide = attns[here, part(i, HD)], weights[side][here, part(at, HD)]
            da[here, part(i, HD)] = ((wide - attn * taken) * scale).astype(BF16)
            one = jnp.sum((wide * attn * scale).reshape(block // 8, 8, HD), 0)
            sums[i] = one if sums[i] is None else sums[i] + one
    gains = [jnp.sum(one, 0, keepdims=True) for one in sums]
    for d in range(quad):
        write_states(outs[d], queries[:, shard_cols(chunk, quad, d, sw)], da[:, part(d, sw)], hs)
        rows_out = gains[d * hs : (d + 1) * hs]
        if last:
            older = [g[part(d, hs), :] for g in gains_before]
            pad = outs[d].shape[0] - sw - (len(older) + 1) * hs
            zero = [jnp.zeros((pad, HD), F32)] if pad else []
            outs[d][sw:, :] = jnp.concatenate(older + rows_out + zero, 0)
        else:
            refs[-1][part(d, hs), :] = jnp.concatenate(rows_out, 0)


def total_kernel(sw, pieces_n, whole, *refs):
    total = refs[0][...]
    for one in refs[1:pieces_n]:
        total = total + one[...]
    refs[pieces_n][...] = total if whole else total[:sw]
    if len(refs) > pieces_n + 1:
        refs[pieces_n + 1][...] = total[sw:]


def give_kernel(sw, quad, later, smalls_n, gate_group, *refs):
    pieces, start, smalls, outs = refs[:quad], refs[quad], refs[quad + 1 : quad + 1 + smalls_n], refs[quad + 1 + smalls_n :]
    member = lax.rem(lax.axis_index("seq"), quad)
    values = [piece[:sw, :] for piece in pieces]
    begin = start[:sw, :]
    if gate_group is not None:
        begin = begin * jnp.where(lax.axis_index("seq") // quad == gate_group, 1.0, 0.0)
    for d in range(quad):
        total = begin
        for e in range(quad):
            if e != d:
                source, target = member ^ e, member ^ d
                take = source > target if later else source < target
                total = total + values[e] * jnp.where(take, 1.0, 0.0)
        outs[d][:sw, :] = total
    if smalls_n:
        small = outs[0].shape[0] - sw
        total = smalls[0][-small:, :]
        for one in smalls[1:]:
            total = total + one[...]
        if gate_group is not None:
            total = total + start[sw:, :]
        for d in range(quad):
            outs[d][sw:, :] = total


def back_kernel(hs, quad, chunk, base, at_side, steps, blk, k, v, da, keep, keep_t, q, gate, attns, weight, inverse, probs, *rest):
    pieces, (gq, ggate, gk, gv) = rest[:steps], rest[steps:]
    rows = keep.shape[0]
    n = rows // blk
    for d in range(steps):
        for h in range(hs):
            mine = part(d * hs + h, HD)
            cols = part((base + d) * hs + h, HD)
            at = head_at(chunk, quad, base + d, hs, h)
            in_side = (at_side + d) * hs + h
            prefix = pieces[d][part(h, HD), :].astype(BF16)
            linear = dot(da[:, cols], prefix, 1, 1)
            dprobs = [
                dot(da[j * blk :, cols], v[part(j, blk), cols], 1, 1).astype(BF16) * keep[j * blk :, part(j, blk)]
                for j in range(n)
            ]
            outs = [dot(dprobs[j], k[part(j, blk), cols], 1, 0) for j in range(n)]
            for i in range(n):
                pieces_q = [linear[part(i, blk)]] + [outs[j][part(i - j, blk)] for j in range(i + 1)]
                gq[part(i, blk), mine] = sum_parts(pieces_q).astype(BF16)
            outs_v, outs_k = [], []
            for j in range(n):
                qs, end = part(j, blk), (j + 1) * blk
                outs_v.append(dot(probs[in_side, packed_rows(j, blk), :], da[qs, cols], 1, 0))
                back = dot(v[:end, cols], da[qs, cols], 1, 1).astype(BF16) * keep_t[:end, qs]
                outs_k.append(dot(back, q[qs, at], 1, 0))
            for i in range(n):
                gv[part(i, blk), mine] = sum_parts([outs_v[j][part(i, blk)] for j in range(i, n)])
                gk[part(i, blk), mine] = sum_parts([outs_k[j][part(i, blk)] for j in range(i, n)])
            sig = jax.nn.sigmoid(gate[:, at].astype(F32))
            ggate[:, mine] = (weight[:, part(in_side, HD)] * attns[:, cols] * inverse[...] * (1.0 - sig)).astype(BF16)


def diagonals(piece, hs, at, d):
    sw = hs * HD
    if hs == 2:
        zero = jnp.zeros((HD, HD), BF16)
        one, two = piece[:HD, :].astype(BF16), piece[HD:sw, :].astype(BF16)
        both = jnp.concatenate([jnp.concatenate([one, zero], 1), jnp.concatenate([zero, two], 1)], 0)
        return [(part(at, sw), part(d, sw), both)]
    return [(part(at * hs + h, HD), part(d * hs + h, HD), piece[part(h, HD), :].astype(BF16)) for h in range(hs)]


def finish_kernel(hs, quad, chunk, chunks, sizes, olds, last, k, v, *rest):
    n = len(sizes)
    sw = hs * HD
    (gq_parts, ggate_parts, gk_parts, gv_parts), rest = [rest[i * n : (i + 1) * n] for i in range(4)], rest[4 * n :]
    pieces, rest = rest[:quad], rest[quad:]
    if last:
        gain, rest = rest[0], rest[1:]
    rest = rest[olds:]
    gq, ggate, gk, gv, rest = *rest[:4], rest[4:]
    if last:
        ggain, rest = rest[0], rest[1:]
    gk_out, gv_out, sems, *rest = rest
    copies = []
    where = [(i, at) for i, size in enumerate(sizes) for at in range(size)]

    def store(d, i, src, dst):
        copy = pltpu.make_async_copy(src, dst.at[:, shard_cols(chunk, quad, d, sw)], sems.at[i, d])
        copy.start()
        copies.append(copy)

    for d in range(quad):
        i, at = where[d]
        store(d, 0, gq_parts[i].at[:, part(at, sw)], gq)
        store(d, 1, ggate_parts[i].at[:, part(at, sw)], ggate)
    if last:
        ggain_out, ggain_sem = rest
        for c in range(chunks):
            for d in range(quad):
                for h in range(hs):
                    at = head_at(c, quad, d, hs, h)
                    row = sw + c * hs + h
                    ggain_out[:, at] = pieces[d][row : row + 1, :] / gain[:, at]
        copy = pltpu.make_async_copy(ggain_out, ggain, ggain_sem.at[0])
        copy.start()
        copies.append(copy)
    for d in range(quad):
        i, at = where[d]
        for mine, cols, suffix in diagonals(pieces[d], hs, at, d):
            gk_out[:, cols] = (gk_parts[i][:, mine] + dot(v[:, cols], suffix, 1, 1)).astype(BF16)
            gv_out[:, cols] = (gv_parts[i][:, mine] + dot(k[:, cols], suffix, 1, 0)).astype(BF16)
        store(d, 2, gk_out.at[:, part(d, sw)], gk)
        store(d, 3, gv_out.at[:, part(d, sw)], gv)
    for copy in copies:
        copy.wait()


def scatter(pieces, count):
    return [pieces[0]] + [
        lax.ppermute(pieces[d], "seq", [(b, b ^ d) for b in range(count)]) for d in range(1, len(pieces))
    ]


def carry(total, count, quad, later):
    groups = count // quad

    def shift(value, by):
        pairs = [(b, b + by * quad) for b in range(count - by * quad)]
        if later:
            pairs = [(t, s) for s, t in pairs]
        return lax.ppermute(value, "seq", pairs)

    if groups == 1:
        return jnp.zeros_like(total)
    total = shift(total, 1)
    by = 1
    while by < groups - 1:
        total = total + shift(total, by)
        by *= 2
    return total


def body(queries, keys, values, gate, grad_out, gain, tile_mask):
    rows, width = queries.shape
    heads = width // HD
    tiles = tile_mask.shape[0]
    tile = rows // tiles
    blk = 2 * tile if tiles % 2 == 0 else tile
    count, head_n = lax.axis_size("seq"), lax.axis_size("head")
    quad = next(g for g in (4, 2, 1) if count % g == 0 and heads % g == 0)
    chunks = 2 if heads % (2 * quad) == 0 else 1
    hs = heads // (quad * chunks)
    sw = hs * HD
    cw = quad * sw
    sides = 2 if quad % 2 == 0 else 1
    steps = quad // sides
    pw = steps * sw
    pad = -(-chunks * hs // 8) * 8
    every = range(chunks)
    final = chunks - 1
    gain_row = gain.reshape(1, width)
    full = float(width * head_n)
    dma = pltpu.SemaphoreType.DMA
    packed = (rows // blk) * (rows // blk + 1) // 2 * blk

    places = [(c, side) for c in every for side in range(sides)]

    def states(c, after):
        first = c == 0
        scratch = [dma((2, quad))]
        scratch += [pltpu.SMEM((tiles, tiles), jnp.int32), dma((1,))] if first else []
        return call(
            functools.partial(states_kernel, quad, hs, c, tiles, tile), "states",
            [(keys, HBM), (values, HBM)] + ([(tile_mask, HBM)] if first else []),
            [(shape((rows, cw), BF16), VMEM)] * 2 + [(shape((sw, HD)), VMEM)] * quad
            + ([(shape((rows, rows), BF16), VMEM)] * 2 if first else []),
            scratch, after,
        )

    def intra(c, side, k, v, after):
        return call(
            functools.partial(intra_kernel, quad, hs, c, side * steps, steps, blk), "intra",
            [(k, VMEM), (v, VMEM), (keep, VMEM), (queries, VMEM), (gate, VMEM), (grad_out, VMEM), (gain_row, VMEM)],
            [(shape((rows, pw)), VMEM)] * 2, [], after,
        )

    def token_sums(c, lots, prefix, before, after):
        extra = [] if before is None else [(before, VMEM)]
        return call(
            functools.partial(sums_kernel, hs, c, before is None, sides, quad), "token_sums",
            [(queries, VMEM)] + [(lot[i], VMEM) for i in (0, 1) for lot in lots] + [(p, VMEM) for p in prefix] + extra,
            [(shape((8, rows)), VMEM), (shape((rows, cw)), VMEM)], (), after, cost=LONG,
        )

    def adjoints(c, attn, parts, gains, after):
        last = c == final
        outs = [(shape((rows, cw), BF16), VMEM)] + ([(shape((rows, HD)), VMEM)] * 2 if c == 0 else [])
        outs += [(shape((sw + (pad if last else 0), HD)), VMEM)] * quad
        if not last:
            outs += [(shape((quad * hs, HD)), VMEM)]
        return call(
            functools.partial(adjoint_kernel, hs, c, full, sides, quad, len(parts), len(gains), last), "adjoints",
            [(queries, VMEM), (attn, VMEM)] + [(lot[1], VMEM) for lot in lots[c]] + [(p, VMEM) for p in parts]
            + [(g, VMEM) for g in gains],
            outs, [], after,
        )

    def probabilities(c, side, k, after):
        return call(
            functools.partial(probs_kernel, hs, quad, c, side * steps, steps, blk), "probs",
            [(k, VMEM), (queries, VMEM), (keep_t, VMEM)], [(shape((steps * hs, packed, blk), BF16), VMEM)], [], after,
        )[0]

    def totals(pieces, whole, after):
        size = pieces[0].shape[0]
        small = 0 if whole else size - sw
        return call(
            functools.partial(total_kernel, sw, quad, whole), "total", [(p, VMEM) for p in pieces],
            [(shape((size if whole else sw, HD)), VMEM)] + ([(shape((small, HD)), VMEM)] if small else []), (), after,
        )

    def give(pieces, start, smalls, later, gate_group, after):
        size = pieces[0].shape[0]
        return call(
            functools.partial(give_kernel, sw, quad, later, len(smalls), gate_group), "give",
            [(p, VMEM) for p in pieces] + [(start, VMEM)] + [(s, VMEM) for s in smalls],
            [(shape((size, HD)), VMEM)] * quad, (), after,
        )

    def back(c, base, size, k, v, da, inverse, prefix, after):
        side = base // steps
        ins = [(k, VMEM), (v, VMEM), (da, VMEM), (keep, VMEM), (keep_t, VMEM), (queries, VMEM), (gate, VMEM)]
        ins += [(attns[c], VMEM), (lots[c][side][1], VMEM), (inverse, VMEM), (probs[(c, side)], VMEM)]
        ins += [(p, VMEM) for p in prefix[base : base + size]]
        return call(
            functools.partial(back_kernel, hs, quad, c, base, base % steps, size, blk), "back", ins,
            [(shape((rows, size * sw), BF16), VMEM)] * 2 + [(shape((rows, size * sw)), VMEM)] * 2, [], after,
        )

    def finish(c, k, v, suffix, outs, after):
        last = c == final
        parts = halves[c]
        ins = [(k, VMEM), (v, VMEM)] + [(p[i], VMEM) for i in range(4) for p in parts] + [(s, VMEM) for s in suffix]
        ins += [(gain_row, VMEM)] if last else []
        aliases = {len(ins) + i: i for i in range(len(outs))}
        sizes = tuple(p[0].shape[1] // sw for p in parts)
        return call(
            functools.partial(finish_kernel, hs, quad, c, chunks, sizes, len(outs), last), "finish",
            ins + [(o, HBM) for o in outs],
            [(shape((rows, width), BF16), HBM)] * 4 + ([(shape((1, width)), HBM)] if last else []),
            [pltpu.VMEM((rows, cw), BF16)] * 2 + [dma((4, quad))]
            + ([pltpu.VMEM((1, width), F32), dma((1,))] if last else []), after, aliases, cost=LONG,
        )

    def scan(messages, later, jobs):
        met = [scatter(m, count) for m in messages]
        done = messages[-1][:1]
        starts, smalls, gates = [], [[] for _ in every], [None for _ in every]
        pair = count == 2 * quad
        for c in every:
            done = jobs(c, done)
            total, *small = totals(met[c], pair, done)
            done = [total]
            if pair:
                starts.append(lax.ppermute(total, "seq", [(b, b ^ quad) for b in range(count)]))
                smalls[c] = [total] if total.shape[0] > sw else []
                gates[c] = 0 if later else 1
                continue
            starts.append(carry(total, count, quad, later))
            if small:
                smalls[c] = small + [
                    lax.ppermute(small[0], "seq", [(b, (b + s * quad) % count) for b in range(count)])
                    for s in range(1, count // quad)
                ]
        gives = []
        for c in every:
            done = jobs(chunks + c, done)
            out = give(met[c], starts[c], smalls[c], later, gates[c], done)
            done = out[:1]
            gives.append(scatter(out, count))
        return gives, jobs(2 * chunks, done)

    kv, messages, after = [], [], []
    for c in every:
        k, v, *pieces = states(c, after)
        if c == 0:
            keep, keep_t = pieces[quad : quad + 2]
        pieces = pieces[:quad]
        after = pieces[:1]
        kv.append((k, v))
        messages.append(pieces)
    lots = [[None] * sides for _ in every]
    def lots_of(items, share):
        cuts, total = [], 0
        for one in share:
            total += one
            cuts.append(round(total * len(items) / sum(share)))
        return [items[i:j] for i, j in zip([0] + cuts, cuts)]

    def windows(share):
        if chunks == 2:
            return share
        return [share[0] + share[1], share[2] + share[3], share[4]]

    intra_lots = lots_of(places, windows(INTRA_SHARE))

    def intra_jobs(window, after):
        for c, side in intra_lots[window]:
            lots[c][side] = intra(c, side, *kv[c], after)
            after = lots[c][side][:1]
        return after

    prefix, after = scan(messages, False, intra_jobs)
    sums, attns, probs = None, [], {}

    def all_probs(picked, after):
        for place in picked:
            probs[place] = probabilities(*place, kv[place[0]][0], after)
            after = [probs[place]]
        return after

    for c in every:
        sums, attn = token_sums(c, lots[c], prefix[c], sums, after)
        attns.append(attn)
        after = all_probs(places[:EARLY_PROBS], [attn]) if c == final - 1 else []
    parts = [sums] + [lax.ppermute(sums, "head", [(b, b ^ d) for b in range(head_n)]) for d in range(1, head_n)]
    after = all_probs([place for place in places if place not in probs], [sums])

    das, messages, gains = [], [], []
    for c in every:
        da, *pieces = adjoints(c, attns[c], parts if c == 0 else scales, gains if c == final else [], after)
        if c == 0:
            scales, pieces = pieces[:2], pieces[2:]
        after = []
        das.append(da)
        messages.append(pieces[:quad])
        gains += pieces[quad:]
    halves = [[] for _ in every]
    back_lots = lots_of([(c, d) for c in every for d in range(quad)], windows(BACK_SHARE))

    def joined(lot):
        out = []
        for c, d in lot:
            if JOIN and out and d % steps and out[-1][0] == c and out[-1][1] + out[-1][2] == d:
                out[-1] = (c, out[-1][1], out[-1][2] + 1)
            else:
                out.append((c, d, 1))
        return out

    def back_jobs(window, after):
        for c, d, size in joined(back_lots[window]):
            halves[c].append(back(c, d, size, *kv[c], das[c], scales[0], prefix[c], after))
            after = halves[c][-1][2:3]
        return after

    suffix, after = scan(messages, True, back_jobs)
    outs = []
    for c in every:
        outs = finish(c, *kv[c], suffix[c], outs[:4], after)
        after = []
    gq, ggate, gk, gv, ggain = outs
    return gq, gk, gv, ggate, ggain.reshape(width)


def solution(mesh):
    spec = P("seq", "head")
    return jax.shard_map(
        body, mesh=mesh, in_specs=(spec,) * 5 + (P("head"), P("seq", None)), out_specs=(spec,) * 4 + (P("head"),),
        check_vma=False,
    )
```
